256 devices in a mesh: src: 32 (over y, x, core), tgt: 8 (over z).
Axes of the slice: x: 4, y: 4, z: 8, core: 2. Of those that a mesh axis runs over, the one named last changes fastest.
Arguments:
- sources: float32 [32768, 128], P(('src', 'tgt')), may hold values from -4 to 4
- targets: float32 [65536, 128], P(('tgt', 'src')), may hold values from -4 to 4
- potential_in: float32 [65536], P('tgt'), may hold values from -1 to 1
Outputs:
- source_potential: float32 [32768], P('src')
- target_potential: float32 [65536], P('tgt')
- mapped: float32 [32768, 128], P(('src', 'tgt'))
The draws below stay inside these ranges and needn't reach their ends.
All inputs are finite; a program needn't handle non-finite values.
Results may differ from the reference program's by a relative error of at most 0.0003.
Values sent between devices are 32-bit elements; how exact they have to be, the bound alone decides.
A program may use at most 128 MiB of HBM per device.

```python
import math
import jax
import jax.numpy as jnp
from jax import lax

FEAT = 128
NS = 32768
NT = 65536


def target_base(key, spread):
    base_key = jax.random.fold_in(key, 11)
    scale_key = jax.random.fold_in(key, 12)
    values = jnp.clip(jax.random.normal(base_key, (NT, FEAT), jnp.float32), -6.0, 6.0) * 0.13
    factors = jnp.exp(jax.random.uniform(scale_key, (NT, 1), jnp.float32) * jnp.log(spread))
    return values * factors


def draw_targets(key, part):
    return target_base(key, 1.0)


def draw_sources(key, part):
    key = jax.random.fold_in(key, 3)
    return jnp.clip(jax.random.normal(key, (NS, FEAT), jnp.float32), -6.0, 6.0) * 0.13


def block_levels(rng, extent, cuts, low, top_value):
    gain, own = 1.0, jax.random.fold_in(rng, 6)
    for position, shards_of in cuts:
        steps = jnp.exp(jax.random.uniform(jax.random.fold_in(own, position), (shards_of,), jnp.float32, low / len(cuts), top_value / len(cuts)))
        gain = gain * jnp.repeat(steps, extent[position] // shards_of).reshape([-1 if axis == position else 1 for axis in range(len(extent))])
    return gain


def centred(rng, extent, scale, limit, pieces=(), kind=jnp.bfloat16):
    array = scale * jax.random.normal(rng, extent, jnp.float32)
    if pieces:
        array = array * block_levels(rng, extent, pieces, -0.22, 0.18)
    return jnp.clip(array, -limit, limit).astype(kind)


def setup_inputs(seed: int = 0) -> dict:
    key_of = jax.random.split(jax.random.key(seed), 4)
    sources = draw_sources(jax.random.fold_in(key_of[3], 71), 0)
    targets = draw_targets(jax.random.fold_in(key_of[3], 71), 0)
    potential_in = centred(key_of[2], (NT,), 0.2, 1.0, ((0, 8),), jnp.float32)
    return {"sources": sources, "targets": targets, "potential_in": potential_in}


epsilon = 0.05


def cost_block(rows_blk, targets, sq_tgt):
    sq_rows = jnp.sum(rows_blk * rows_blk, axis=1)
    inner = jnp.dot(rows_blk, targets.T, precision=lax.Precision.HIGHEST, preferred_element_type=jnp.float32)
    return sq_rows[:, None] + sq_tgt[None, :] - 2.0 * inner


def reference(sources, targets, potential_in):
    num_src = sources.shape[0]
    num_tgt = targets.shape[0]
    width = sources.shape[1]
    block_rows = math.gcd(num_src, 256)
    nblocks = num_src // block_rows
    src_blocks = sources.reshape(nblocks, block_rows, width)
    sq_tgt = jnp.sum(targets * targets, axis=1)

    def row_pass(rows_blk):
        scores = (potential_in[None, :] - cost_block(rows_blk, targets, sq_tgt)) / epsilon
        top = jnp.max(scores, axis=1)
        return top + jnp.log(jnp.sum(jnp.exp(scores - top[:, None]), axis=1))

    row_lse = lax.map(row_pass, src_blocks).reshape(num_src)
    source_potential = -epsilon * jnp.log(jnp.float32(num_src)) - epsilon * row_lse
    pot_blocks = source_potential.reshape(nblocks, block_rows)

    def column_step(running, inputs):
        rows_blk, pot_blk = inputs
        scores = (pot_blk[:, None] - cost_block(rows_blk, targets, sq_tgt)) / epsilon
        top = jnp.max(scores, axis=0)
        total = jnp.sum(jnp.exp(scores - top[None, :]), axis=0)
        new_top = jnp.maximum(running[0], top)
        new_total = running[1] * jnp.exp(running[0] - new_top) + total * jnp.exp(top - new_top)
        return (new_top, new_total), None

    start = (jnp.full((num_tgt,), -jnp.inf, jnp.float32), jnp.zeros((num_tgt,), jnp.float32))
    (col_top, col_total), _ = lax.scan(column_step, start, (src_blocks, pot_blocks))
    target_potential = -epsilon * jnp.log(jnp.float32(num_tgt)) - epsilon * (col_top + jnp.log(col_total))

    def map_pass(rows_blk):
        scores = (target_potential[None, :] - cost_block(rows_blk, targets, sq_tgt)) / epsilon
        top = jnp.max(scores, axis=1)
        weights = jnp.exp(scores - top[:, None])
        total = jnp.sum(weights, axis=1)
        summed = jnp.dot(weights, targets, precision=lax.Precision.HIGHEST, preferred_element_type=jnp.float32)
        return summed / total[:, None]

    mapped = lax.map(map_pass, src_blocks).reshape(num_src, width)
    return source_potential, target_potential, mapped
```

```python
import math

import jax
import jax.numpy as jnp
from jax import lax
from jax.experimental import pallas as pl
from jax.experimental.pallas import tpu as pltpu
from jax.sharding import PartitionSpec as P

epsilon = 0.05
LN2 = math.log(2.0)
ALPHA = 1.0 / (epsilon * LN2)
MESH = pl.DeviceIdType.MESH
F32 = jnp.float32
BF16 = jnp.bfloat16
NSRC = 32
NTGT = 8
SIDE = 4
PAIR = 2 * SIDE
LAG = 3
ORDER = (1, 7, 2, 6, 0, 4, 3, 5)
EARLY = 640


def gray(i):
    return i + i // 2 - 2 * (i // 3)


def kernel(
    src_ref, tgt_ref, pot_ref, sp_ref, tp_ref, map_ref,
    sbuf, tbuf, lhs, cols, scores, top, total, rslot, rrow, rcol,
    lsend, lrecv, call, colmax, acc, den, psend, msend, precv, mrecv,
    z_send, z_recv, p1_send, p2_send, half_send, sib_send, t_recv, sib_recv,
    r_send, r_recv, l_send, l_recv, c_send, c_recv, m_send, m_recv,
):
    me = lax.axis_index("src")
    z = lax.axis_index("tgt")
    core = me % 2
    chip = me // 2
    x = chip % SIDE
    y = chip // SIDE
    sib = me + 1 - 2 * core

    def on_src(i):
        return {"src": i}

    def on_tgt(i):
        return {"tgt": (i + NTGT) % NTGT}

    def rcopy(src, dst, send, recv, dev):
        return pltpu.make_async_remote_copy(
            src_ref=src, dst_ref=dst, send_sem=send, recv_sem=recv, device_id=dev, device_id_type=MESH
        )

    bar = pltpu.get_barrier_semaphore()

    def greet_src(i, carry):
        pl.semaphore_signal(bar, inc=1, device_id=on_src((me + i) % NSRC), device_id_type=MESH)
        return carry

    def greet_tgt(i, carry):
        pl.semaphore_signal(bar, inc=1, device_id=on_tgt(z + i), device_id_type=MESH)
        return carry

    lax.fori_loop(1, NSRC, greet_src, 0)
    lax.fori_loop(1, NTGT, greet_tgt, 0)

    for h in range(2):
        tbuf[chip, core, h] = tgt_ref[pl.ds(h * 128, 128), :]
    sbuf[0] = src_ref[...]

    lane = lax.broadcasted_iota(jnp.int32, (128, 128), 1)
    row = lax.broadcasted_iota(jnp.int32, (128, 128), 0)
    eye = lane == row

    def split3(a):
        a1 = a.astype(BF16).astype(F32)
        rest = a - a1
        a2 = rest.astype(BF16).astype(F32)
        return a1, a2, rest - a2

    def prep_src(place, d):
        s = sbuf[d]
        scaled = s * (2.0 * ALPHA)
        hi = scaled.astype(BF16)
        lo = (scaled - hi.astype(F32)).astype(BF16)
        b1, b2, b3 = split3(-ALPHA * jnp.sum(s * s, axis=1, keepdims=True))
        extra = jnp.where(lane == 0, b1, jnp.where(lane == 1, b2, jnp.where(lane == 2, b3, jnp.where(lane < 6, 1.0, 0.0))))
        rows = pl.ds(place * 128, 128)
        lhs[rows, 0:128] = hi
        lhs[rows, 128:256] = hi
        lhs[rows, 256:384] = lo
        lhs[rows, 384:512] = extra.astype(BF16)

    def prep_tgt(u, q, h):
        for c in range(2):
            t = tbuf[q, c, h]
            pot = pot_ref[pl.ds(q * 4 + c * 2 + h, 1), :]
            hi = t.astype(BF16)
            lo = (t - hi.astype(F32)).astype(BF16)
            a1, a2, a3 = split3(ALPHA * jnp.sum(jnp.where(eye, pot, 0.0) - t * t, axis=1, keepdims=True))
            extra = jnp.where(lane < 3, 1.0, jnp.where(lane == 3, a1, jnp.where(lane == 4, a2, jnp.where(lane == 5, a3, 0.0))))
            rows = pl.ds(c * 128, 128)
            cols[u, rows, 0:128] = lo
            cols[u, rows, 128:256] = hi
            cols[u, rows, 256:384] = hi
            cols[u, rows, 384:512] = extra.astype(BF16)

    prep_src(ORDER.index(0), 0)
    top[...] = jnp.full((1024, 128), -jnp.inf, F32)
    total[...] = jnp.zeros((1024, 128), F32)
    pl.semaphore_wait(bar, NSRC + NTGT - 2)

    def at(xx, yy):
        return (((yy + SIDE) % SIDE) * SIDE + (xx + SIDE) % SIDE) * 2 + core

    def p1_copy(h, i):
        step = 1 - 2 * i
        dev = on_src(at(x + step * (1 - h), y + step * h))
        piece = tbuf.at[chip, core, h]
        return rcopy(piece, piece, p1_send.at[h * 2 + i], t_recv.at[0, h * 16 + chip], dev)

    def z_copy(hop, i):
        d = (NTGT - hop) % NTGT if i == 0 else hop
        to = (d + NTGT - 1) % NTGT if i == 0 else (d + 1) % NTGT
        dev = on_tgt(z + 1 if i == 0 else z - 1)
        if hop < 3:
            return rcopy(sbuf.at[d], sbuf.at[to], z_send.at[hop * 2 + i], z_recv.at[to], dev)
        rows = pl.ds(i * 64, 64)
        return rcopy(sbuf.at[d, rows], sbuf.at[to, rows], z_send.at[hop * 2 + i], z_recv.at[to + 4 * i], dev)

    for h in range(2):
        for i in range(2):
            p1_copy(h, i).start()
    for i in range(2):
        z_copy(0, i).start()

    def z_arrive(hop):
        if hop < 4:
            for i, d in enumerate((NTGT - hop, hop)):
                rcopy(sbuf.at[d], sbuf.at[d], z_send.at[0], z_recv.at[d], on_tgt(z + 1)).wait_recv()
                z_copy(hop, i).start()
            for d in (NTGT - hop, hop):
                prep_src(ORDER.index(d), d)
        else:
            for i in range(2):
                part = sbuf.at[4, pl.ds(i * 64, 64)]
                rcopy(part, part, z_send.at[0], z_recv.at[4 + 4 * i], on_tgt(z + 1)).wait_recv()
            prep_src(ORDER.index(4), 4)

    def place_of(m, h):
        late = (m + 12) // 16
        d1 = gray((1 - late) * m + late * ((m + 8) // 3 - 4))
        d2 = gray(late * ((m + 8) % 3 + 1))
        dx = (1 - h) * d1 + h * d2
        dy = (1 - h) * d2 + h * d1
        q = ((y + dy) % SIDE) * SIDE + (x + dx) % SIDE
        return d1, d2, q

    def p2_copy(m, h, q, i):
        step = 1 - 2 * i
        dev = on_src(at(x + step * h, y + step * (1 - h)))
        piece = tbuf.at[q, core, h]
        return rcopy(piece, piece, p2_send.at[m * 4 + h * 2 + i], t_recv.at[0, h * 16 + q], dev)

    def half_copy(m, h, q, d1, d2):
        d = d1 + d2 if isinstance(d1, int) else d1 * (1 - (d2 + 3) // 4) + d2
        second = (d2 + 3) // 4
        step = d - 2
        axis = (second + h) % 2
        part = (3 - d) // 2
        dev = on_src(at(x + step * (1 - axis), y + step * axis))
        piece = tbuf.at[q, core, h, pl.ds(pl.multiple_of(part * 64, 64), 64)]
        return rcopy(piece, piece, half_send.at[m * 2 + h], t_recv.at[part, h * 16 + q], dev)

    def sib_copy(m, h, q):
        piece = tbuf.at[q, core, h]
        return rcopy(piece, piece, sib_send.at[m * 2 + h], sib_recv.at[h * 16 + q], on_src(sib))

    def is_half(d1, d2):
        return (d2 % 2) + (1 - (d2 + 3) // 4) * (d1 % 2)

    def in_parts(d1, d2):
        return (d2 // 2) * (1 - d2 % 2) + (1 - (d2 + 3) // 4) * (d1 // 2) * (1 - d1 % 2)

    def gather_step(m):
        for h in range(2):
            d1, d2, q = place_of(m, h)
            parts = in_parts(d1, d2)
            piece = tbuf.at[q, core, h]

            @pl.when(jnp.logical_and(m > 0, parts == 0))
            def _():
                rcopy(piece, piece, sib_send.at[0], t_recv.at[0, h * 16 + q], on_src(sib)).wait_recv()

            @pl.when(parts == 1)
            def _():
                for i in range(2):
                    part = tbuf.at[q, core, h, pl.ds(i * 64, 64)]
                    rcopy(part, part, sib_send.at[0], t_recv.at[i, h * 16 + q], on_src(sib)).wait_recv()

            @pl.when(is_half(d1, d2) == 1)
            def _():
                half_copy(m, h, q, d1, d2).start()

            @pl.when(m < 4)
            def _():
                for i in range(2):
                    p2_copy(m, h, q, i).start()

            sib_copy(m, h, q).start()

    def score_rows(m, r0, n):
        us = []
        for h in range(2):
            _, _, q = place_of(m, h)
            u = q * 2 + h
            us.append(u)
            scores[u, pl.ds(r0, n), :] = lax.dot_general(
                lhs[pl.ds(r0, n), :], cols[u], (((1,), (1,)), ((), ())), preferred_element_type=F32
            )
        for r in range(r0, r0 + n, 64):
            rows = pl.ds(r, 64)
            parts = [scores[u, rows, pl.ds(k * 128, 128)] for u in us for k in range(2)]
            old = top[rows, :]
            new = jnp.maximum(jnp.maximum(parts[0], parts[1]), jnp.maximum(parts[2], parts[3]))
            new = jnp.maximum(old, new)
            e = [jnp.exp2(p - new) for p in parts]
            total[rows, :] = total[rows, :] * jnp.exp2(old - new) + ((e[0] + e[1]) + (e[2] + e[3]))
            top[rows, :] = new

    def first_pass(m, carry):
        @pl.when(m < 16)
        def _():
            gather_step(m)

        for hop in range(1, 5):

            @pl.when(m == hop - 1)
            def _():
                z_arrive(hop)

        p = m - 2

        @pl.when(p >= 0)
        def _():
            for h in range(2):
                _, _, q = place_of(p, h)
                piece = tbuf.at[q, 1 - core, h]
                rcopy(piece, piece, sib_send.at[0], sib_recv.at[h * 16 + q], on_src(sib)).wait_recv()
                prep_tgt(q * 2 + h, q, h)
            score_rows(p, 0, EARLY)

        @pl.when(p >= PAIR)
        def _():
            def both(i, c):
                score_rows(p - PAIR + PAIR * i, EARLY, 1024 - EARLY)
                return c

            lax.fori_loop(0, 2, both, 0)

        return carry

    lax.fori_loop(0, 18, first_pass, 0)

    for place, d in enumerate(ORDER):
        rows = pl.ds(place * 128, 128)
        m = top[rows, :]
        high = jnp.max(m, axis=1, keepdims=True)
        s = jnp.sum(total[rows, :] * jnp.exp2(m - high), axis=1, keepdims=True)
        r = high + jnp.log2(s)
        rslot[z, pl.ds((z + d) % NTGT, 1), :] = jnp.sum(jnp.where(eye, r, 0.0), axis=0, keepdims=True)

    def r_copy(i):
        return rcopy(rslot.at[z], rslot.at[z], r_send.at[i], r_recv.at[z], on_tgt(z + i))

    for i in range(1, NTGT):
        r_copy(i).start()

    for h in range(2):
        for i in range(2):
            p1_copy(h, i).wait_send()
    for hop in range(4):
        for i in range(2):
            z_copy(hop, i).wait_send()

    def gather_sent(m, carry):
        for h in range(2):
            d1, d2, q = place_of(m, h)

            @pl.when(is_half(d1, d2) == 1)
            def _():
                half_copy(m, h, q, d1, d2).wait_send()

            @pl.when(m < 4)
            def _():
                for i in range(2):
                    p2_copy(m, h, q, i).wait_send()

            sib_copy(m, h, q).wait_send()
        return carry

    lax.fori_loop(0, 16, gather_sent, 0)

    for i in range(1, NTGT):
        other = (z + i) % NTGT
        slot = rslot.at[other]
        rcopy(slot, slot, r_send.at[0], r_recv.at[other], on_tgt(z + i)).wait_recv()
    slots = [rslot[i] for i in range(NTGT)]
    high = slots[0]
    for s in slots[1:]:
        high = jnp.maximum(high, s)
    sums = jnp.exp2(slots[0] - high)
    for s in slots[1:]:
        sums = sums + jnp.exp2(s - high)
    r_all = high + jnp.log2(sums)
    rrow[...] = r_all
    sp_ref[...] = -epsilon * math.log(NSRC * 1024) - (epsilon * LN2) * r_all
    for place, d in enumerate(ORDER):
        one = rrow[pl.ds((z + d) % NTGT, 1), :]
        rcol[pl.ds(place * 128, 128), :] = jnp.transpose(jnp.broadcast_to(one, (128, 128)))

    def l_copy(u):
        return rcopy(lsend.at[u], lrecv.at[me], l_send.at[u], l_recv.at[me], on_src(u))

    def c_copy(i):
        return rcopy(call.at[me], call.at[me], c_send.at[i], c_recv.at[me], on_src((me + i) % NSRC))

    def column_unit(u):
        step = 32
        high = None
        for r in range(0, 1024, step):
            rows = pl.ds(r, step)
            rc = rcol[rows, :]
            v = [scores[u, rows, pl.ds(k * 128, 128)] - rc for k in range(2)]
            high = v if high is None else [jnp.maximum(a, b) for a, b in zip(high, v)]
        high = [jnp.max(a, axis=0, keepdims=True) for a in high]
        sums = None
        for r in range(0, 1024, step):
            rows = pl.ds(r, step)
            rc = rcol[rows, :]
            e = [jnp.exp2((scores[u, rows, pl.ds(k * 128, 128)] - rc) - high[k]) for k in range(2)]
            for k in range(2):
                scores[u, rows, pl.ds(k * 128, 128)] = e[k]
            sums = e if sums is None else [a + b for a, b in zip(sums, e)]
        for k in range(2):
            part = pl.ds(k * 128, 128)
            colmax[u, :, part] = high[k]
            lsend[u, :, part] = high[k] + jnp.log2(jnp.sum(sums[k], axis=0, keepdims=True))

        @pl.when(u != me)
        def _():
            l_copy(u).start()

        @pl.when(u == me)
        def _():
            lrecv[me] = lsend[u]

    def column_total():
        def arrived(i, carry):
            other = (me + i) % NSRC
            slot = lrecv.at[other]
            rcopy(slot, slot, l_send.at[0], l_recv.at[other], on_src(other)).wait_recv()
            return carry

        lax.fori_loop(1, NSRC, arrived, 0)
        parts = lrecv[...]
        high = jnp.max(parts, axis=0)
        call[me] = high + jnp.log2(jnp.sum(jnp.exp2(parts - high[None]), axis=0))

        def tell(i, carry):
            c_copy(i).start()
            return carry

        lax.fori_loop(1, NSRC, tell, 0)

    def second_pass(k, carry):
        @pl.when(k < NSRC)
        def _():
            column_unit(k)

        @pl.when(k == me + LAG)
        def _():
            column_total()

        return carry

    lax.fori_loop(0, NSRC + LAG, second_pass, 0)

    def map_group(r0, first):
        rows = pl.ds(r0, 256)
        acc[...] = jnp.zeros((256, 256), F32)
        den[...] = jnp.zeros((256, 128), F32)

        def unit(u, carry):
            if first:

                @pl.when(u != me)
                def _():
                    slot = call.at[u]
                    rcopy(slot, slot, c_send.at[0], c_recv.at[u], on_src(u)).wait_recv()

            f = jnp.exp2(colmax[u] - call[u])
            w = scores[u, rows, :] * f
            den[...] += w[:, :128] + w[:, 128:]
            hi = w.astype(BF16)
            lo = (w - hi.astype(F32)).astype(BF16)
            t = cols[u, :, 0:256]
            acc[...] += jnp.dot(hi, t, preferred_element_type=F32) + jnp.dot(lo, t, preferred_element_type=F32)
            return carry

        lax.fori_loop(0, NSRC, unit, 0)
        out = []
        for i in range(2):
            part = pl.ds(i * 128, 128)
            d = jnp.sum(den[part, :], axis=1, keepdims=True)
            out.append((acc[part, 0:128] + acc[part, 128:256], jnp.sum(jnp.where(eye, d, 0.0), axis=0, keepdims=True)))
        return out

    def put(buf, pair, extra=None, lo=0, hi=136):
        num, d = pair
        d = jnp.broadcast_to(d, (8, 128))
        if extra is None:
            buf[0:128, :] = num
            buf[128:136, :] = d
            return
        if lo == 0:
            n = min(hi, 128)
            buf[0:n, :] = num[0:n] + extra[0:n, :]
            if n < 128:
                buf[n:128, :] = num[n:128]
        else:
            buf[0:lo, :] = num[0:lo]
            buf[lo:128, :] = num[lo:128] + extra[lo:128, :]
        buf[128:136, :] = d + extra[128:136, :] if hi == 136 else d

    halves = (pl.ds(0, 64), pl.ds(64, 72))

    def plus(hop):
        rows = halves[0] if hop == 0 else pl.ds(0, 136)
        return rcopy(psend.at[hop, rows], precv.at[hop, rows], m_send.at[hop], m_recv.at[hop], on_tgt(z + 1))

    def minus(hop):
        rows = halves[1] if hop == 0 else pl.ds(0, 136)
        return rcopy(msend.at[hop, rows], mrecv.at[hop, rows], m_send.at[4 + hop], m_recv.at[4 + hop], on_tgt(z - 1))

    own, far = map_group(512, True)
    put(psend.at[0], far)
    put(msend.at[0], far)
    plus(0).start()
    minus(0).start()
    for hop, r0 in ((1, 768), (2, 256), (3, 0)):
        if hop == 1:
            own_num, own_den = own
            acc_own = own_num
        up, down = map_group(r0, False)
        plus(hop - 1).wait_recv()
        if hop == 1:
            put(psend.at[hop], up, precv.at[hop - 1], 0, 64)
        else:
            put(psend.at[hop], up, precv.at[hop - 1])
        plus(hop).start()
        minus(hop - 1).wait_recv()
        if hop == 1:
            put(msend.at[hop], down, mrecv.at[hop - 1], 64, 136)
        else:
            put(msend.at[hop], down, mrecv.at[hop - 1])
        minus(hop).start()

    for u in range(NSRC):
        for c in range(2):
            r = (u // 2) * 4 + c * 2 + u % 2
            tp_ref[r : r + 1, :] = (
                pot_ref[r : r + 1, :] - (epsilon * LN2) * call[u, :, c * 128 : (c + 1) * 128]
                - epsilon * math.log(NTGT * 8192 / (NSRC * 1024))
            )
    for i in range(1, NTGT):
        r_copy(i).wait_send()

    def small_sent(i, carry):
        c_copy(i).wait_send()
        l_copy((me + i) % NSRC).wait_send()
        return carry

    lax.fori_loop(1, NSRC, small_sent, 0)
    for hop in range(4):
        plus(hop).wait_send()
        minus(hop).wait_send()
    plus(3).wait_recv()
    minus(3).wait_recv()
    num = acc_own + precv[3, 0:128, :] + mrecv[3, 0:128, :]
    d = own_den + precv[3, 128:129, :] + mrecv[3, 128:129, :]
    d = jnp.sum(jnp.where(eye, d, 0.0), axis=1, keepdims=True)
    map_ref[...] = num / d


def per_device(sources, targets, potential_in):
    vmem = pl.BlockSpec(memory_space=pltpu.VMEM)
    dma = pltpu.SemaphoreType.DMA
    sp, tp, mapped = pl.pallas_call(
        kernel,
        out_shape=(
            jax.ShapeDtypeStruct((8, 128), F32),
            jax.ShapeDtypeStruct((64, 128), F32),
            jax.ShapeDtypeStruct((128, 128), F32),
        ),
        in_specs=[vmem] * 3,
        out_specs=(vmem,) * 3,
        scratch_shapes=[
            pltpu.VMEM((8, 128, 128), F32),
            pltpu.VMEM((16, 2, 2, 128, 128), F32),
            pltpu.VMEM((1024, 512), BF16),
            pltpu.VMEM((32, 256, 512), BF16),
            pltpu.VMEM((32, 1024, 256), F32),
            pltpu.VMEM((1024, 128), F32),
            pltpu.VMEM((1024, 128), F32),
            pltpu.VMEM((8, 8, 128), F32),
            pltpu.VMEM((8, 128), F32),
            pltpu.VMEM((1024, 128), F32),
            pltpu.VMEM((32, 1, 256), F32),
            pltpu.VMEM((32, 1, 256), F32),
            pltpu.VMEM((32, 1, 256), F32),
            pltpu.VMEM((32, 1, 256), F32),
            pltpu.VMEM((256, 256), F32),
            pltpu.VMEM((256, 128), F32),
            pltpu.VMEM((4, 136, 128), F32),
            pltpu.VMEM((4, 136, 128), F32),
            pltpu.VMEM((4, 136, 128), F32),
            pltpu.VMEM((4, 136, 128), F32),
            dma((8,)),
            dma((9,)),
            dma((4,)),
            dma((16,)),
            dma((32,)),
            dma((32,)),
            dma((2, 32)),
            dma((32,)),
            dma((8,)),
            dma((8,)),
            dma((32,)),
            dma((32,)),
            dma((32,)),
            dma((32,)),
            dma((8,)),
            dma((8,)),
        ],
        compiler_params=pltpu.CompilerParams(
            collective_id=0, has_side_effects=True, vmem_limit_bytes=62 * 1024 * 1024
        ),
        cost_estimate=pl.CostEstimate(
            flops=2 * 1024 * 8192 * 1024, bytes_accessed=1 << 20, transcendentals=2 * 1024 * 8192
        ),
    )(sources, targets, potential_in.reshape(64, 128))
    return sp.reshape(1024), tp.reshape(8192), mapped


def solution(mesh):
    return jax.shard_map(
        per_device,
        mesh=mesh,
        in_specs=(P(("src", "tgt"), None), P(("tgt", "src"), None), P("tgt")),
        out_specs=(P("src"), P("tgt"), P(("src", "tgt"), None)),
        check_vma=False,
    )
```

```python
import math

import jax
import jax.numpy as jnp
from jax import lax
from jax.experimental import pallas as pl
from jax.experimental.pallas import tpu as pltpu
from jax.sharding import PartitionSpec as P

epsilon = 0.05
LN2 = math.log(2.0)
ALPHA = 1.0 / (epsilon * LN2)
MESH = pl.DeviceIdType.MESH
F32 = jnp.float32
BF16 = jnp.bfloat16
NSRC = 32
NTGT = 8
WIDE = 4
SIDE = 4
PAIR = 2 * SIDE
LAG = 16
ORDER = (1, 7, 2, 6, 0, 4, 3, 5)
EARLY = 640


STEPS = (
    (0, 0), (1, 0), (3, 0), (2, 0), (0, 1), (0, 3), (1, 1), (1, 3),
    (3, 1), (3, 3), (0, 2), (1, 2), (2, 1), (2, 3), (3, 2), (2, 2),
)
HALVED = (10, 11, 14)


def look_up(m, values):
    found = values[0]
    for k in range(1, len(values)):
        found = jnp.where(m == k, values[k], found)
    return found


def kernel(
    src_ref, tgt_ref, pot_ref, sp_ref, tp_ref, map_ref,
    sbuf, tbuf, lhs, cols, scores, top, total, rslot, rrow, rcol,
    lsend, lrecv, call, colmax, acc, den, zsend, zland,
    z_send, z_recv, p1_send, p2_send, half_send, sib_send, t_recv, sib_recv,
    r_send, r_recv, l_send, l_recv, c_send, c_recv, m_send, m_recv,
):
    me = lax.axis_index("src")
    z = lax.axis_index("tgt")
    core = me % 2
    chip = me // 2
    x = chip % SIDE
    y = chip // SIDE
    sib = me + 1 - 2 * core

    def on_src(i):
        return {"src": i}

    def on_tgt(i):
        return {"tgt": (i + NTGT) % NTGT}

    def rcopy(src, dst, send, recv, dev):
        return pltpu.make_async_remote_copy(
            src_ref=src, dst_ref=dst, send_sem=send, recv_sem=recv, device_id=dev, device_id_type=MESH
        )

    bar = pltpu.get_barrier_semaphore()

    def greet_src(i, carry):
        pl.semaphore_signal(bar, inc=1, device_id=on_src((me + i) % NSRC), device_id_type=MESH)
        return carry

    def greet_tgt(i, carry):
        pl.semaphore_signal(bar, inc=1, device_id=on_tgt(z + i), device_id_type=MESH)
        return carry

    lax.fori_loop(1, NSRC, greet_src, 0)
    lax.fori_loop(1, NTGT, greet_tgt, 0)

    for h in range(2):
        tbuf[chip, core, h] = tgt_ref[pl.ds(h * 128, 128), :]
    sbuf[0] = src_ref[...]

    lane = lax.broadcasted_iota(jnp.int32, (128, 128), 1)
    row = lax.broadcasted_iota(jnp.int32, (128, 128), 0)
    eye = lane == row

    def split3(a):
        a1 = a.astype(BF16).astype(F32)
        rest = a - a1
        a2 = rest.astype(BF16).astype(F32)
        return a1, a2, rest - a2

    def prep_src(place, d):
        s = sbuf[d]
        scaled = s * (2.0 * ALPHA)
        hi = scaled.astype(BF16)
        lo = (scaled - hi.astype(F32)).astype(BF16)
        b1, b2, b3 = split3(-ALPHA * jnp.sum(s * s, axis=1, keepdims=True))
        extra = jnp.where(lane == 0, b1, jnp.where(lane == 1, b2, jnp.where(lane == 2, b3, jnp.where(lane < 6, 1.0, 0.0))))
        rows = pl.ds(place * 128, 128)
        lhs[rows, 0:128] = hi
        lhs[rows, 128:256] = hi
        lhs[rows, 256:384] = lo
        lhs[rows, 384:512] = extra.astype(BF16)

    def prep_tgt(u, q, h):
        for c in range(2):
            t = tbuf[q, c, h]
            pot = pot_ref[pl.ds(q * 4 + c * 2 + h, 1), :]
            hi = t.astype(BF16)
            lo = (t - hi.astype(F32)).astype(BF16)
            a1, a2, a3 = split3(ALPHA * jnp.sum(jnp.where(eye, pot, 0.0) - t * t, axis=1, keepdims=True))
            extra = jnp.where(lane < 3, 1.0, jnp.where(lane == 3, a1, jnp.where(lane == 4, a2, jnp.where(lane == 5, a3, 0.0))))
            rows = pl.ds(c * 128, 128)
            cols[u, rows, 0:128] = lo
            cols[u, rows, 128:256] = hi
            cols[u, rows, 256:384] = hi
            cols[u, rows, 384:512] = extra.astype(BF16)

    prep_src(ORDER.index(0), 0)
    top[...] = jnp.full((1024, 128), -jnp.inf, F32)
    total[...] = jnp.zeros((1024, 128), F32)
    pl.semaphore_wait(bar, NSRC + NTGT - 2)

    def at(xx, yy):
        return (((yy + SIDE) % SIDE) * SIDE + (xx + SIDE) % SIDE) * 2 + core

    def step_of(i):
        return (1, -1, 2)[i]

    def p1_copy(h, i):
        step = step_of(i)
        dev = on_src(at(x + step * (1 - h), y + step * h))
        piece = tbuf.at[chip, core, h]
        return rcopy(piece, piece, p1_send.at[h * 3 + i], t_recv.at[0, h * 16 + chip], dev)

    def z_copy(n):
        up = n % 2 == 0
        sign = 1 if up else -1
        if n < 4:
            d, to, far = 0, (-sign * (1 + n // 2)) % NTGT, 1 + n // 2
        elif n < 6:
            d, to, far = (-2 * sign) % NTGT, (-3 * sign) % NTGT, 1
        else:
            rows = pl.ds(0 if up else 64, 64)
            d = (-2 * sign) % NTGT
            return rcopy(sbuf.at[d, rows], sbuf.at[4, rows], z_send.at[n], z_recv.at[4 if up else 8], on_tgt(z + 2 * sign))
        return rcopy(sbuf.at[d], sbuf.at[to], z_send.at[n], z_recv.at[to], on_tgt(z + far * sign))

    for i in range(3):
        for h in range(2):
            p1_copy(h, i).start()
    for n in (2, 3, 0, 1):
        z_copy(n).start()

    def z_wait(d):
        rcopy(sbuf.at[d], sbuf.at[d], z_send.at[0], z_recv.at[d], on_tgt(z + 1)).wait_recv()

    def z_near():
        for d, n in ((6, 4), (2, 5)):
            z_wait(d)
            z_copy(n).start()
            z_copy(n + 2).start()
        for d in (6, 2):
            prep_src(ORDER.index(d), d)

    def z_next():
        for d in (7, 1):
            z_wait(d)
            prep_src(ORDER.index(d), d)

    def z_late():
        for d in (5, 3):
            z_wait(d)
            prep_src(ORDER.index(d), d)
        for i in range(2):
            part = sbuf.at[4, pl.ds(i * 64, 64)]
            rcopy(part, part, z_send.at[0], z_recv.at[4 + 4 * i], on_tgt(z + 1)).wait_recv()
        prep_src(ORDER.index(4), 4)

    def place_of(m, h):
        code = look_up(m, [a * 4 + b for a, b in STEPS])
        d1 = code // 4
        d2 = code % 4
        dx = (1 - h) * d1 + h * d2
        dy = (1 - h) * d2 + h * d1
        return d2, ((y + dy) % SIDE) * SIDE + (x + dx) % SIDE

    def p2_copy(m, h, q, i):
        step = step_of(i)
        dev = on_src(at(x + step * h, y + step * (1 - h)))
        piece = tbuf.at[q, core, h]
        return rcopy(piece, piece, p2_send.at[m * 6 + h * 3 + i], t_recv.at[0, h * 16 + q], dev)

    def half_copy(m, h, q, d2):
        step = d2 - 2
        part = (3 - d2) // 2
        dev = on_src(at(x + step * h, y + step * (1 - h)))
        piece = tbuf.at[q, core, h, pl.ds(pl.multiple_of(part * 64, 64), 64)]
        return rcopy(piece, piece, half_send.at[(m - 4) * 2 + h], t_recv.at[part, h * 16 + q], dev)

    def sib_copy(m, h, q):
        piece = tbuf.at[q, core, h]
        return rcopy(piece, piece, sib_send.at[m * 2 + h], sib_recv.at[h * 16 + q], on_src(sib))

    def handed_on(m):
        return jnp.logical_and(m >= 4, m < 10)

    def gather_step(m):
        halved = look_up(m, [int(k in HALVED) for k in range(16)])
        for h in range(2):
            d2, q = place_of(m, h)
            piece = tbuf.at[q, core, h]

            @pl.when(jnp.logical_and(m > 0, halved == 0))
            def _():
                rcopy(piece, piece, sib_send.at[0], t_recv.at[0, h * 16 + q], on_src(sib)).wait_recv()

            @pl.when(halved == 1)
            def _():
                for i in range(2):
                    part = tbuf.at[q, core, h, pl.ds(i * 64, 64)]
                    rcopy(part, part, sib_send.at[0], t_recv.at[i, h * 16 + q], on_src(sib)).wait_recv()

            @pl.when(handed_on(m))
            def _():
                half_copy(m, h, q, d2).start()

            @pl.when(m < 4)
            def _():
                for i in range(2):
                    p2_copy(m, h, q, i).start()

            @pl.when(m == 3)
            def _():
                p2_copy(m, h, q, 2).start()

            sib_copy(m, h, q).start()

    def score_rows(m, r0, n):
        us = []
        for h in range(2):
            _, q = place_of(m, h)
            u = q * 2 + h
            us.append(u)
            scores[u, pl.ds(r0, n), :] = lax.dot_general(
                lhs[pl.ds(r0, n), :], cols[u], (((1,), (1,)), ((), ())), preferred_element_type=F32
            )
        for r in range(r0, r0 + n, 64):
            rows = pl.ds(r, 64)
            parts = [scores[u, rows, pl.ds(k * 128, 128)] for u in us for k in range(2)]
            old = top[rows, :]
            new = jnp.maximum(jnp.maximum(parts[0], parts[1]), jnp.maximum(parts[2], parts[3]))
            new = jnp.maximum(old, new)
            e = [jnp.exp2(p - new) for p in parts]
            total[rows, :] = total[rows, :] * jnp.exp2(old - new) + ((e[0] + e[1]) + (e[2] + e[3]))
            top[rows, :] = new

    def first_pass(m, carry):
        @pl.when(m < 16)
        def _():
            gather_step(m)

        for n, action in ((1, z_near), (2, z_next), (10, z_late)):

            @pl.when(m == n)
            def _():
                action()

        p = m - 2

        @pl.when(p >= 0)
        def _():
            for h in range(2):
                _, q = place_of(p, h)
                piece = tbuf.at[q, 1 - core, h]
                rcopy(piece, piece, sib_send.at[0], sib_recv.at[h * 16 + q], on_src(sib)).wait_recv()
                prep_tgt(q * 2 + h, q, h)
            score_rows(p, 0, EARLY)

        @pl.when(p >= PAIR)
        def _():
            def both(i, c):
                score_rows(p - PAIR + PAIR * i, EARLY, 1024 - EARLY)
                return c

            lax.fori_loop(0, 2, both, 0)

        return carry

    lax.fori_loop(0, 18, first_pass, 0)

    for place, d in enumerate(ORDER):
        rows = pl.ds(place * 128, 128)
        m = top[rows, :]
        high = jnp.max(m, axis=1, keepdims=True)
        s = jnp.sum(total[rows, :] * jnp.exp2(m - high), axis=1, keepdims=True)
        r = high + jnp.log2(s)
        rslot[z, pl.ds((z + d) % NTGT, 1), :] = jnp.sum(jnp.where(eye, r, 0.0), axis=0, keepdims=True)

    def r_copy(i):
        return rcopy(rslot.at[z], rslot.at[z], r_send.at[i], r_recv.at[z], on_tgt(z + i))

    for i in range(1, NTGT):
        r_copy(i).start()

    for h in range(2):
        for i in range(3):
            p1_copy(h, i).wait_send()
    for n in range(8):
        z_copy(n).wait_send()

    def gather_sent(m, carry):
        for h in range(2):
            d2, q = place_of(m, h)

            @pl.when(handed_on(m))
            def _():
                half_copy(m, h, q, d2).wait_send()

            @pl.when(m < 4)
            def _():
                for i in range(2):
                    p2_copy(m, h, q, i).wait_send()

            @pl.when(m == 3)
            def _():
                p2_copy(m, h, q, 2).wait_send()

            sib_copy(m, h, q).wait_send()
        return carry

    lax.fori_loop(0, 16, gather_sent, 0)

    for i in range(1, NTGT):
        other = (z + i) % NTGT
        slot = rslot.at[other]
        rcopy(slot, slot, r_send.at[0], r_recv.at[other], on_tgt(z + i)).wait_recv()
    slots = [rslot[i] for i in range(NTGT)]
    high = slots[0]
    for s in slots[1:]:
        high = jnp.maximum(high, s)
    sums = jnp.exp2(slots[0] - high)
    for s in slots[1:]:
        sums = sums + jnp.exp2(s - high)
    r_all = high + jnp.log2(sums)
    rrow[...] = r_all
    sp_ref[...] = -epsilon * math.log(NSRC * 1024) - (epsilon * LN2) * r_all
    for place, d in enumerate(ORDER):
        one = rrow[pl.ds((z + d) % NTGT, 1), :]
        rcol[pl.ds(place * 128, 128), :] = jnp.transpose(jnp.broadcast_to(one, (128, 128)))

    def l_copy(u):
        return rcopy(lsend.at[u], lrecv.at[me], l_send.at[u], l_recv.at[me], on_src(u))

    def c_copy(i):
        return rcopy(call.at[me], call.at[me], c_send.at[i], c_recv.at[me], on_src((me + i) % NSRC))

    def column_unit(u):
        for k in range(2):
            lanes = pl.ds(k * 128, 128)
            tops, sums = [], []
            for b in range(8):
                rows = pl.ds(b * 128, 128)
                v = scores[u, rows, lanes] - rcol[rows, :]
                q = jnp.max(v, axis=0, keepdims=True)
                e = jnp.exp2(v - q)
                scores[u, rows, lanes] = e
                tops.append(q)
                sums.append(jnp.sum(e, axis=0, keepdims=True))
            tops = jnp.concatenate(tops, axis=0)
            sums = jnp.concatenate(sums, axis=0)
            colmax[u, :, lanes] = tops
            high = jnp.max(tops, axis=0, keepdims=True)
            lsend[u, :, lanes] = high + jnp.log2(jnp.sum(sums * jnp.exp2(tops - high), axis=0, keepdims=True))

        @pl.when(u != me)
        def _():
            l_copy(u).start()

        @pl.when(u == me)
        def _():
            lrecv[me] = lsend[u]

    def column_total():
        def arrived(i, carry):
            other = (me + i) % NSRC
            slot = lrecv.at[other]
            rcopy(slot, slot, l_send.at[0], l_recv.at[other], on_src(other)).wait_recv()
            return carry

        lax.fori_loop(1, NSRC, arrived, 0)
        parts = lrecv[...]
        high = jnp.max(parts, axis=0)
        call[me] = high + jnp.log2(jnp.sum(jnp.exp2(parts - high[None]), axis=0))

        def tell(i, carry):
            c_copy(i).start()
            return carry

        lax.fori_loop(1, NSRC, tell, 0)

    def second_pass(k, carry):
        column_unit(k)

        @pl.when(k == me + LAG)
        def _():
            column_total()

        return carry

    lax.fori_loop(0, NSRC, second_pass, 0)

    @pl.when(me + LAG >= NSRC)
    def _():
        column_total()

    acc[...] = jnp.zeros((1024, 256), F32)
    den[...] = jnp.zeros((1024, 128), F32)

    def map_units(i, r0, n, wait):
        if wait:
            for j in range(WIDE):
                u = i * WIDE + j

                @pl.when(u != me)
                def _():
                    slot = call.at[u]
                    rcopy(slot, slot, c_send.at[0], c_recv.at[u], on_src(u)).wait_recv()

        high, low, t, sums = [], [], [], None
        for j in range(WIDE):
            u = i * WIDE + j
            f = jnp.exp2(colmax[u] - call[u])
            ws = [scores[u, pl.ds(b * 128, 128), :] * f[b : b + 1, :] for b in range(r0 // 128, (r0 + n) // 128)]
            w = jnp.concatenate(ws, axis=0)
            half = w[:, :128] + w[:, 128:]
            sums = half if sums is None else sums + half
            hi = w.astype(BF16)
            high.append(hi)
            low.append((w - hi.astype(F32)).astype(BF16))
            t.append(cols[u, :, 0:256])
        rows = pl.ds(r0, n)
        den[rows, :] += sums
        acc[rows, :] += jnp.dot(
            jnp.concatenate(high + low, axis=1), jnp.concatenate(t + t, axis=0), preferred_element_type=F32
        )

    def map_rows(first, last, r0, n, wait):
        def body(i, carry):
            map_units(i, r0, n, wait)
            return carry

        lax.fori_loop(first // WIDE, last // WIDE, body, 0)

    def block(place):
        rows = pl.ds(place * 128, 128)
        d = jnp.sum(den[rows, :], axis=1, keepdims=True)
        return acc[rows, 0:128] + acc[rows, 128:256], jnp.sum(jnp.where(eye, d, 0.0), axis=0, keepdims=True)

    def z_sum(n):
        sign = 1 if n % 2 == 0 else -1
        rows = pl.ds(0, 136) if n >= 2 else (pl.ds(0, 64) if n == 0 else pl.ds(64, 72))
        far = (2, 1, 2, 1)[n // 2]
        return rcopy(zsend.at[n, rows], zland.at[n, rows], m_send.at[n], m_recv.at[n], on_tgt(z + far * sign))

    def put(n, place):
        num, d = block(place)
        zsend[n, 0:128, :] = num
        zsend[n, 128:136, :] = jnp.broadcast_to(d, (8, 128))

    map_rows(0, LAG, 0, 1024, True)
    map_rows(LAG, NSRC, EARLY, 1024 - EARLY, True)
    for n, d in ((0, 4), (1, 4), (2, 3), (3, 5)):
        put(n, ORDER.index(d))
        z_sum(n).start()
    map_rows(LAG, NSRC, 0, EARLY, False)
    for n, d in ((6, 1), (7, 7)):
        put(n, ORDER.index(d))
        z_sum(n).start()
    for n, d in ((4, 2), (5, 6)):
        put(n, ORDER.index(d))
        for k in (n - 4, n - 2):
            z_sum(k).wait_recv()
        zsend[n] += zland[n - 2]
        part = pl.ds(0, 64) if n == 4 else pl.ds(64, 72)
        zsend[n, part, :] += zland[n - 4, part, :]
        z_sum(n).start()
    own_num, own_den = block(ORDER.index(0))

    for u in range(NSRC):
        for c in range(2):
            r = (u // 2) * 4 + c * 2 + u % 2
            tp_ref[r : r + 1, :] = (
                pot_ref[r : r + 1, :] - (epsilon * LN2) * call[u, :, c * 128 : (c + 1) * 128]
                - epsilon * math.log(NTGT * 8192 / (NSRC * 1024))
            )
    for i in range(1, NTGT):
        r_copy(i).wait_send()

    def small_sent(i, carry):
        c_copy(i).wait_send()
        l_copy((me + i) % NSRC).wait_send()
        return carry

    lax.fori_loop(1, NSRC, small_sent, 0)
    for n in range(8):
        z_sum(n).wait_send()
    for n in range(4, 8):
        z_sum(n).wait_recv()
    num = (own_num + (zland[6, 0:128, :] + zland[7, 0:128, :])) + (zland[4, 0:128, :] + zland[5, 0:128, :])
    d = (own_den + (zland[6, 128:129, :] + zland[7, 128:129, :])) + (zland[4, 128:129, :] + zland[5, 128:129, :])
    d = jnp.sum(jnp.where(eye, d, 0.0), axis=1, keepdims=True)
    map_ref[...] = num / d


def finish(sp, tp, mapped, sp_ref, tp_ref, map_ref):
    sp_ref[...] = sp[...]
    tp_ref[...] = tp[...]
    map_ref[...] = mapped[...]


def per_device(sources, targets, potential_in):
    vmem = pl.BlockSpec(memory_space=pltpu.VMEM)
    dma = pltpu.SemaphoreType.DMA
    shapes = (
        jax.ShapeDtypeStruct((8, 128), F32),
        jax.ShapeDtypeStruct((64, 128), F32),
        jax.ShapeDtypeStruct((128, 128), F32),
    )
    results = pl.pallas_call(
        kernel,
        out_shape=shapes,
        in_specs=[vmem] * 3,
        out_specs=(vmem,) * 3,
        scratch_shapes=[
            pltpu.VMEM((8, 128, 128), F32),
            pltpu.VMEM((16, 2, 2, 128, 128), F32),
            pltpu.VMEM((1024, 512), BF16),
            pltpu.VMEM((32, 256, 512), BF16),
            pltpu.VMEM((32, 1024, 256), F32),
            pltpu.VMEM((1024, 128), F32),
            pltpu.VMEM((1024, 128), F32),
            pltpu.VMEM((8, 8, 128), F32),
            pltpu.VMEM((8, 128), F32),
            pltpu.VMEM((1024, 128), F32),
            pltpu.VMEM((32, 1, 256), F32),
            pltpu.VMEM((32, 1, 256), F32),
            pltpu.VMEM((32, 1, 256), F32),
            pltpu.VMEM((32, 8, 256), F32),
            pltpu.VMEM((1024, 256), F32),
            pltpu.VMEM((1024, 128), F32),
            pltpu.VMEM((8, 136, 128), F32),
            pltpu.VMEM((8, 136, 128), F32),
            dma((8,)),
            dma((9,)),
            dma((6,)),
            dma((24,)),
            dma((12,)),
            dma((32,)),
            dma((2, 32)),
            dma((32,)),
            dma((8,)),
            dma((8,)),
            dma((32,)),
            dma((32,)),
            dma((32,)),
            dma((32,)),
            dma((8,)),
            dma((8,)),
        ],
        compiler_params=pltpu.CompilerParams(
            collective_id=0, has_side_effects=True, vmem_limit_bytes=62 * 1024 * 1024
        ),
        cost_estimate=pl.CostEstimate(
            flops=2 * 1024 * 8192 * 1024, bytes_accessed=1 << 20, transcendentals=2 * 1024 * 8192
        ),
    )(sources, targets, potential_in.reshape(64, 128))
    sp, tp, mapped = pl.pallas_call(
        finish, out_shape=shapes, in_specs=[vmem] * 3, out_specs=(vmem,) * 3
    )(*results)
    return sp.reshape(1024), tp.reshape(8192), mapped


def solution(mesh):
    return jax.shard_map(
        per_device,
        mesh=mesh,
        in_specs=(P(("src", "tgt"), None), P(("tgt", "src"), None), P("tgt")),
        out_specs=(P("src"), P("tgt"), P(("src", "tgt"), None)),
        check_vma=False,
    )
```

```python
import math

import jax
import jax.numpy as jnp
from jax import lax
from jax.experimental import pallas as pl
from jax.experimental.pallas import tpu as pltpu
from jax.sharding import PartitionSpec as P

epsilon = 0.05
LN2 = math.log(2.0)
ALPHA = 1.0 / (epsilon * LN2)
MESH = pl.DeviceIdType.MESH
F32 = jnp.float32
BF16 = jnp.bfloat16
NSRC = 32
NTGT = 8
ORDER = (4, 3, 5, 1, 7, 0, 2, 6)
SIDE = 4
WIDE = 8
AHEAD = 2
EARLY = 5


def gray(i):
    return i + i // 2 - 2 * (i // 3)


def kernel(
    src_ref, tgt_ref, pot_ref, sp_ref, tp_ref, map_ref,
    sbuf, tbuf, lhs, cols, scores, top, total, rslot, rcol,
    lsend, lrecv, call, colmax, acc, den, zsend, zland, colsum,
    z_send, z_recv, p1_send, p2_send, sib_send, t_recv, sib_recv,
    r_send, r_recv, l_send, l_recv, c_send, c_recv, m_send, m_recv,
):
    me = lax.axis_index("src")
    z = lax.axis_index("tgt")
    core = me % 2
    chip = me // 2
    x = chip % SIDE
    y = chip // SIDE
    sib = me + 1 - 2 * core

    def on_src(i):
        return {"src": i}

    def on_tgt(i):
        return {"tgt": (i + NTGT) % NTGT}

    def rcopy(src, dst, send, recv, dev):
        return pltpu.make_async_remote_copy(
            src_ref=src, dst_ref=dst, send_sem=send, recv_sem=recv, device_id=dev, device_id_type=MESH
        )

    bar = pltpu.get_barrier_semaphore()

    def greet_src(i, carry):
        pl.semaphore_signal(bar, inc=1, device_id=on_src((me + i) % NSRC), device_id_type=MESH)
        return carry

    def greet_tgt(i, carry):
        pl.semaphore_signal(bar, inc=1, device_id=on_tgt(z + i), device_id_type=MESH)
        return carry

    lax.fori_loop(1, NSRC, greet_src, 0)
    lax.fori_loop(1, NTGT, greet_tgt, 0)

    for h in range(2):
        tbuf[chip, core, h] = tgt_ref[pl.ds(h * 128, 128), :]
    sbuf[0] = src_ref[...]

    lane = lax.broadcasted_iota(jnp.int32, (128, 128), 1)
    row = lax.broadcasted_iota(jnp.int32, (128, 128), 0)
    eye = lane == row

    def split3(a):
        a1 = a.astype(BF16).astype(F32)
        rest = a - a1
        a2 = rest.astype(BF16).astype(F32)
        return a1, a2, rest - a2

    def prep_src(d):
        s = sbuf[d]
        scaled = s * (2.0 * ALPHA)
        hi = scaled.astype(BF16)
        lo = (scaled - hi.astype(F32)).astype(BF16)
        b1, b2, b3 = split3(-ALPHA * jnp.sum(s * s, axis=1, keepdims=True))
        extra = jnp.where(lane == 0, b1, jnp.where(lane == 1, b2, jnp.where(lane == 2, b3, jnp.where(lane < 6, 1.0, 0.0))))
        rows = pl.ds(pl.multiple_of((z + d) % NTGT * 128, 128), 128)
        lhs[rows, 0:128] = hi
        lhs[rows, 128:256] = hi
        lhs[rows, 256:384] = lo
        lhs[rows, 384:512] = extra.astype(BF16)

    def prep_tgt(u, q, h):
        for c in range(2):
            t = tbuf[q, c, h]
            pot = pot_ref[pl.ds(q * 4 + c * 2 + h, 1), :]
            hi = t.astype(BF16)
            lo = (t - hi.astype(F32)).astype(BF16)
            a1, a2, a3 = split3(ALPHA * jnp.sum(jnp.where(eye, pot, 0.0) - t * t, axis=1, keepdims=True))
            extra = jnp.where(lane < 3, 1.0, jnp.where(lane == 3, a1, jnp.where(lane == 4, a2, jnp.where(lane == 5, a3, 0.0))))
            rows = pl.ds(c * 128, 128)
            cols[u, rows, 0:128] = lo
            cols[u, rows, 128:256] = hi
            cols[u, rows, 256:384] = hi
            cols[u, rows, 384:512] = extra.astype(BF16)

    prep_src(0)
    top[...] = jnp.full((1024, 128), -jnp.inf, F32)
    total[...] = jnp.zeros((1024, 128), F32)
    pl.semaphore_wait(bar, NSRC + NTGT - 2)

    def at(xx, yy):
        return (((yy + SIDE) % SIDE) * SIDE + (xx + SIDE) % SIDE) * 2 + core

    def step_of(i):
        return (1, -1, 2)[i]

    def p1_copy(h, i):
        step = step_of(i)
        dev = on_src(at(x + step * (1 - h), y + step * h))
        piece = tbuf.at[chip, core, h]
        return rcopy(piece, piece, p1_send.at[h * 3 + i], t_recv.at[h * 16 + chip], dev)

    def z_copy(n):
        up = n % 2 == 0
        sign = 1 if up else -1
        if n < 4:
            d, to, far = 0, (-sign * (1 + n // 2)) % NTGT, 1 + n // 2
        elif n < 6:
            d, to, far = (-2 * sign) % NTGT, (-3 * sign) % NTGT, 1
        else:
            rows = pl.ds(0 if up else 64, 64)
            d = (-2 * sign) % NTGT
            return rcopy(sbuf.at[d, rows], sbuf.at[4, rows], z_send.at[n], z_recv.at[4 if up else 8], on_tgt(z + 2 * sign))
        return rcopy(sbuf.at[d], sbuf.at[to], z_send.at[n], z_recv.at[to], on_tgt(z + far * sign))

    for i in range(3):
        for h in range(2):
            p1_copy(h, i).start()
    for n in (2, 3, 0, 1):
        z_copy(n).start()

    def z_wait(d):
        rcopy(sbuf.at[d], sbuf.at[d], z_send.at[0], z_recv.at[d], on_tgt(z + 1)).wait_recv()

    def z_near():
        for d, n in ((6, 4), (2, 5)):
            z_wait(d)
            z_copy(n).start()
            z_copy(n + 2).start()
        for d in (6, 2):
            prep_src(d)

    def z_next():
        for d in (7, 1):
            z_wait(d)
            prep_src(d)

    def z_late():
        for d in (5, 3):
            z_wait(d)
            prep_src(d)
        for i in range(2):
            part = sbuf.at[4, pl.ds(i * 64, 64)]
            rcopy(part, part, z_send.at[0], z_recv.at[4 + 4 * i], on_tgt(z + 1)).wait_recv()
        prep_src(4)

    def place_of(m, h):
        g1 = jnp.where(m < 4, m, (m + 8) // 3 - 4)
        g2 = jnp.where(m < 4, 0, (m + 8) % 3 + 1)
        d1, d2 = gray(g1), gray(g2)
        dx = (1 - h) * d1 + h * d2
        dy = (1 - h) * d2 + h * d1
        return ((y + dy) % SIDE) * SIDE + (x + dx) % SIDE

    def slot_of(u):
        q, h = u // 2, u % 2
        dx = (q % SIDE - x + SIDE) % SIDE
        dy = (q // SIDE - y + SIDE) % SIDE
        g1 = gray(jnp.where(h == 0, dx, dy))
        g2 = gray(jnp.where(h == 0, dy, dx))
        return 2 * jnp.where(g2 == 0, g1, 3 + 3 * g1 + g2) + h

    def p2_copy(m, h, q, i):
        step = step_of(i)
        dev = on_src(at(x + step * h, y + step * (1 - h)))
        piece = tbuf.at[q, core, h]
        return rcopy(piece, piece, p2_send.at[m * 6 + h * 3 + i], t_recv.at[h * 16 + q], dev)

    def sib_copy(m, h, q):
        piece = tbuf.at[q, core, h]
        return rcopy(piece, piece, sib_send.at[m * 2 + h], sib_recv.at[h * 16 + q], on_src(sib))

    def gather_step(m):
        for h in range(2):
            q = place_of(m, h)
            piece = tbuf.at[q, core, h]

            @pl.when(m > 0)
            def _():
                rcopy(piece, piece, sib_send.at[0], t_recv.at[h * 16 + q], on_src(sib)).wait_recv()

            @pl.when(m < 4)
            def _():
                for i in range(3):
                    p2_copy(m, h, q, i).start()

            sib_copy(m, h, q).start()

    def score_rows(us, r0, n):
        for u in us:
            scores[u, pl.ds(r0, n), :] = lax.dot_general(
                lhs[pl.ds(r0, n), :], cols[u], (((1,), (1,)), ((), ())), preferred_element_type=F32
            )
        for r in range(r0, r0 + n, 64):
            rows = pl.ds(r, 64)
            parts = [scores[u, rows, pl.ds(k * 128, 128)] for u in us for k in range(2)]
            old = top[rows, :]
            new = old
            for p in parts:
                new = jnp.maximum(new, p)
            sums = total[rows, :] * jnp.exp2(old - new)
            for p in parts:
                sums = sums + jnp.exp2(p - new)
            total[rows, :] = sums
            top[rows, :] = new

    def lead(m, carry):
        gather_step(m)

        @pl.when(m == 2)
        def _():
            z_near()

        return carry

    lax.fori_loop(0, 4, lead, 0)
    z_next()
    z_late()

    def first_pass(p, carry):
        m = p + AHEAD

        @pl.when(jnp.logical_and(m >= 4, m < 16))
        def _():
            gather_step(m)

        for h in range(2):
            q = place_of(p, h)
            piece = tbuf.at[q, 1 - core, h]
            rcopy(piece, piece, sib_send.at[0], sib_recv.at[h * 16 + q], on_src(sib)).wait_recv()
        for h in range(2):
            prep_tgt(p * 2 + h, place_of(p, h), h)
        score_rows((p * 2, p * 2 + 1), 0, EARLY * 128)
        return carry

    lax.fori_loop(0, 16, first_pass, 0)

    def r_copy(part, i):
        slot = rslot.at[part, z]
        return rcopy(slot, slot, r_send.at[part * NTGT + i], r_recv.at[part * NTGT + z], on_tgt(z + i))

    def row_sums(part, blocks):
        rslot[part, z] = jnp.zeros((8, 128), F32)
        for c in blocks:
            rows = pl.ds(c * 128, 128)
            m = top[rows, :]
            high = jnp.max(m, axis=1, keepdims=True)
            s = jnp.sum(total[rows, :] * jnp.exp2(m - high), axis=1, keepdims=True)
            r = high + jnp.log2(s)
            rslot[part, z, c : c + 1, :] = jnp.sum(jnp.where(eye, r, 0.0), axis=0, keepdims=True)
        for i in range(1, NTGT):
            r_copy(part, i).start()

    def row_totals(part, blocks):
        for i in range(1, NTGT):
            other = (z + i) % NTGT
            slot = rslot.at[part, other]
            rcopy(slot, slot, r_send.at[0], r_recv.at[part * NTGT + other], on_tgt(z + i)).wait_recv()
        slots = [rslot[part, i] for i in range(NTGT)]
        high = slots[0]
        for s in slots[1:]:
            high = jnp.maximum(high, s)
        sums = jnp.exp2(slots[0] - high)
        for s in slots[1:]:
            sums = sums + jnp.exp2(s - high)
        r_all = high + jnp.log2(sums)
        for c in blocks:
            one = r_all[c : c + 1, :]
            sp_ref[c : c + 1, :] = -epsilon * math.log(NSRC * 1024) - (epsilon * LN2) * one
            rcol[pl.ds(c * 128, 128), :] = jnp.transpose(jnp.broadcast_to(one, (128, 128)))

    early, late = range(EARLY), range(EARLY, 8)
    row_sums(0, early)

    def late_rows(i, carry):
        score_rows([i * 4 + j for j in range(4)], EARLY * 128, 1024 - EARLY * 128)
        return carry

    lax.fori_loop(0, 8, late_rows, 0)
    row_sums(1, late)

    for h in range(2):
        for i in range(3):
            p1_copy(h, i).wait_send()
    for n in range(8):
        z_copy(n).wait_send()

    def gather_sent(m, carry):
        for h in range(2):
            q = place_of(m, h)

            @pl.when(m < 4)
            def _():
                for i in range(3):
                    p2_copy(m, h, q, i).wait_send()

            sib_copy(m, h, q).wait_send()
        return carry

    lax.fori_loop(0, 16, gather_sent, 0)
    row_totals(0, early)

    def l_copy(u):
        return rcopy(lsend.at[u], lrecv.at[me], l_send.at[u], l_recv.at[me], on_src(u))

    def c_copy(i):
        return rcopy(call.at[me], call.at[me], c_send.at[i], c_recv.at[me], on_src((me + i) % NSRC))

    def column_blocks(slot, blocks):
        b0, n = blocks[0], len(blocks)
        for k in range(2):
            lanes = pl.ds(k * 128, 128)
            tops, sums = [], []
            for b in blocks:
                rows = pl.ds(b * 128, 128)
                v = scores[slot, rows, lanes] - rcol[rows, :]
                q = jnp.max(v, axis=0, keepdims=True)
                e = jnp.exp2(v - q)
                scores[slot, rows, lanes] = e
                tops.append(q)
                sums.append(jnp.sum(e, axis=0, keepdims=True))
            colmax[slot, pl.ds(b0, n), lanes] = jnp.concatenate(tops, axis=0)
            colsum[slot, pl.ds(b0, n), lanes] = jnp.concatenate(sums, axis=0)

    def early_blocks(slot, carry):
        column_blocks(slot, early)
        return carry

    def late_blocks(u, carry):
        slot = slot_of(u)
        column_blocks(slot, late)
        tops = colmax[slot]
        high = jnp.max(tops, axis=0, keepdims=True)
        lsend[u] = high + jnp.log2(jnp.sum(colsum[slot] * jnp.exp2(tops - high), axis=0, keepdims=True))

        @pl.when(u != me)
        def _():
            l_copy(u).start()

        @pl.when(u == me)
        def _():
            lrecv[me] = lsend[u]

        return carry

    def column_total():
        def arrived(i, carry):
            other = (me + i) % NSRC
            slot = lrecv.at[other]
            rcopy(slot, slot, l_send.at[0], l_recv.at[other], on_src(other)).wait_recv()
            return carry

        lax.fori_loop(1, NSRC, arrived, 0)
        parts = lrecv[...]
        high = jnp.max(parts, axis=0)
        call[me] = high + jnp.log2(jnp.sum(jnp.exp2(parts - high[None]), axis=0))

        def tell(i, carry):
            c_copy(i).start()
            return carry

        lax.fori_loop(1, NSRC, tell, 0)

    lax.fori_loop(0, NSRC, early_blocks, 0)
    row_totals(1, late)
    lax.fori_loop(0, NSRC, late_blocks, 0)
    column_total()

    acc[...] = jnp.zeros((1024, 256), F32)
    den[...] = jnp.zeros((1024, 128), F32)

    def map_units(i, dists, wait):
        if wait:
            for j in range(WIDE):
                u = i * WIDE + j

                @pl.when(u != me)
                def _():
                    slot = call.at[u]
                    rcopy(slot, slot, c_send.at[0], c_recv.at[u], on_src(u)).wait_recv()

        high, low, t, sums = [], [], [], None
        for j in range(WIDE):
            u = i * WIDE + j
            slot = slot_of(u)
            ws = []
            for d in dists:
                c = (z + d) % NTGT
                f = jnp.exp2(colmax[slot, pl.ds(c, 1), :] - call[u])
                ws.append(scores[slot, pl.ds(pl.multiple_of(c * 128, 128), 128), :] * f)
            w = jnp.concatenate(ws, axis=0)
            half = w[:, :128] + w[:, 128:]
            sums = half if sums is None else sums + half
            hi = w.astype(BF16)
            high.append(hi)
            low.append((w - hi.astype(F32)).astype(BF16))
            t.append(cols[slot, :, 0:256])
        rows = pl.ds(ORDER.index(dists[0]) * 128, len(dists) * 128)
        den[rows, :] += sums
        acc[rows, :] += jnp.dot(
            jnp.concatenate(high + low, axis=1), jnp.concatenate(t + t, axis=0), preferred_element_type=F32
        )

    def map_rows(dists, wait):
        def body(i, carry):
            map_units(i, dists, wait)
            return carry

        lax.fori_loop(0, NSRC // WIDE, body, 0)

    def block(place):
        rows = pl.ds(place * 128, 128)
        d = jnp.sum(den[rows, :], axis=1, keepdims=True)
        return acc[rows, 0:128] + acc[rows, 128:256], jnp.sum(jnp.where(eye, d, 0.0), axis=0, keepdims=True)

    def z_sum(n):
        sign = 1 if n % 2 == 0 else -1
        rows = pl.ds(0, 136) if n >= 2 else (pl.ds(0, 64) if n == 0 else pl.ds(64, 72))
        far = (2, 1, 2, 1)[n // 2]
        return rcopy(zsend.at[n, rows], zland.at[n, rows], m_send.at[n], m_recv.at[n], on_tgt(z + far * sign))

    def put(n, place):
        num, d = block(place)
        zsend[n, 0:128, :] = num
        zsend[n, 128:136, :] = jnp.broadcast_to(d, (8, 128))

    map_rows(ORDER[0:3], True)
    for n, d in ((0, 4), (1, 4), (2, 3), (3, 5)):
        put(n, ORDER.index(d))
        z_sum(n).start()
    map_rows(ORDER[3:6], False)
    for n, d in ((6, 1), (7, 7)):
        put(n, ORDER.index(d))
        z_sum(n).start()
    map_rows(ORDER[6:8], False)
    for n, d in ((4, 2), (5, 6)):
        put(n, ORDER.index(d))
        for k in (n - 4, n - 2):
            z_sum(k).wait_recv()
        zsend[n] += zland[n - 2]
        part = pl.ds(0, 64) if n == 4 else pl.ds(64, 72)
        zsend[n, part, :] += zland[n - 4, part, :]
        z_sum(n).start()
    own_num, own_den = block(ORDER.index(0))

    for u in range(NSRC):
        for c in range(2):
            r = (u // 2) * 4 + c * 2 + u % 2
            tp_ref[r : r + 1, :] = (
                pot_ref[r : r + 1, :] - (epsilon * LN2) * call[u, :, c * 128 : (c + 1) * 128]
                - epsilon * math.log(NTGT * 8192 / (NSRC * 1024))
            )
    for i in range(1, NTGT):
        for part in range(2):
            r_copy(part, i).wait_send()

    def small_sent(i, carry):
        c_copy(i).wait_send()
        l_copy((me + i) % NSRC).wait_send()
        return carry

    lax.fori_loop(1, NSRC, small_sent, 0)
    for n in range(8):
        z_sum(n).wait_send()
    for n in range(4, 8):
        z_sum(n).wait_recv()
    num = (own_num + (zland[6, 0:128, :] + zland[7, 0:128, :])) + (zland[4, 0:128, :] + zland[5, 0:128, :])
    d = (own_den + (zland[6, 128:129, :] + zland[7, 128:129, :])) + (zland[4, 128:129, :] + zland[5, 128:129, :])
    d = jnp.sum(jnp.where(eye, d, 0.0), axis=1, keepdims=True)
    map_ref[...] = num / d


def finish(sp, tp, mapped, sp_ref, tp_ref, map_ref):
    sp_ref[...] = sp[...]
    tp_ref[...] = tp[...]
    map_ref[...] = mapped[...]


def per_device(sources, targets, potential_in):
    vmem = pl.BlockSpec(memory_space=pltpu.VMEM)
    dma = pltpu.SemaphoreType.DMA
    shapes = (
        jax.ShapeDtypeStruct((8, 128), F32),
        jax.ShapeDtypeStruct((64, 128), F32),
        jax.ShapeDtypeStruct((128, 128), F32),
    )
    results = pl.pallas_call(
        kernel,
        out_shape=shapes,
        in_specs=[vmem] * 3,
        out_specs=(vmem,) * 3,
        scratch_shapes=[
            pltpu.VMEM((8, 128, 128), F32),
            pltpu.VMEM((16, 2, 2, 128, 128), F32),
            pltpu.VMEM((1024, 512), BF16),
            pltpu.VMEM((32, 256, 512), BF16),
            pltpu.VMEM((32, 1024, 256), F32),
            pltpu.VMEM((1024, 128), F32),
            pltpu.VMEM((1024, 128), F32),
            pltpu.VMEM((2, 8, 8, 128), F32),
            pltpu.VMEM((1024, 128), F32),
            pltpu.VMEM((32, 1, 256), F32),
            pltpu.VMEM((32, 1, 256), F32),
            pltpu.VMEM((32, 1, 256), F32),
            pltpu.VMEM((32, 8, 256), F32),
            pltpu.VMEM((1024, 256), F32),
            pltpu.VMEM((1024, 128), F32),
            pltpu.VMEM((8, 136, 128), F32),
            pltpu.VMEM((8, 136, 128), F32),
            pltpu.VMEM((32, 8, 256), F32),
            dma((8,)),
            dma((9,)),
            dma((6,)),
            dma((24,)),
            dma((32,)),
            dma((32,)),
            dma((32,)),
            dma((16,)),
            dma((16,)),
            dma((32,)),
            dma((32,)),
            dma((32,)),
            dma((32,)),
            dma((8,)),
            dma((8,)),
        ],
        compiler_params=pltpu.CompilerParams(
            collective_id=0, has_side_effects=True, vmem_limit_bytes=62 * 1024 * 1024
        ),
        cost_estimate=pl.CostEstimate(
            flops=2 * 1024 * 8192 * 1024, bytes_accessed=1 << 20, transcendentals=2 * 1024 * 8192
        ),
    )(sources, targets, potential_in.reshape(64, 128))
    sp, tp, mapped = pl.pallas_call(
        finish, out_shape=shapes, in_specs=[vmem] * 3, out_specs=(vmem,) * 3
    )(*results)
    return sp.reshape(1024), tp.reshape(8192), mapped


def solution(mesh):
    return jax.shard_map(
        per_device,
        mesh=mesh,
        in_specs=(P(("src", "tgt"), None), P(("tgt", "src"), None), P("tgt")),
        out_specs=(P("src"), P("tgt"), P(("src", "tgt"), None)),
        check_vma=False,
    )
```

```python
import math

import jax
import jax.numpy as jnp
from jax import lax
from jax.experimental import pallas as pl
from jax.experimental.pallas import tpu as pltpu
from jax.sharding import PartitionSpec as P

epsilon = 0.05
LN2 = math.log(2.0)
ALPHA = 1.0 / (epsilon * LN2)
MESH = pl.DeviceIdType.MESH
F32 = jnp.float32
BF16 = jnp.bfloat16
NSRC = 32
NTGT = 8
ORDER = (4, 3, 5, 1, 7, 0, 2, 6)
SIDE = 4
WIDE = 8
EARLY = 5


def gray(i):
    return i + i // 2 - 2 * (i // 3)


def kernel(
    src_ref, tgt_ref, pot_ref, sp_ref, tp_ref, map_ref,
    sbuf, tbuf, lhs, cols, scores, top, total, rslot, rcol,
    lsend, lrecv, call, colmax, acc, den, zsend, zland, colsum,
    in_sem, z_send, z_recv, p1_send, p2_send, sib_send, t_recv, sib_recv,
    r_send, r_recv, l_send, l_recv, c_send, c_recv, m_send, m_recv,
):
    me = lax.axis_index("src")
    z = lax.axis_index("tgt")
    core = me % 2
    chip = me // 2
    x = chip % SIDE
    y = chip // SIDE
    sib = me + 1 - 2 * core

    def on_src(i):
        return {"src": i}

    def on_tgt(i):
        return {"tgt": (i + NTGT) % NTGT}

    def rcopy(src, dst, send, recv, dev):
        return pltpu.make_async_remote_copy(
            src_ref=src, dst_ref=dst, send_sem=send, recv_sem=recv, device_id=dev, device_id_type=MESH
        )

    bar = pltpu.get_barrier_semaphore()

    def greet_src(i, carry):
        pl.semaphore_signal(bar, inc=1, device_id=on_src((me + i) % NSRC), device_id_type=MESH)
        return carry

    def greet_tgt(i, carry):
        pl.semaphore_signal(bar, inc=1, device_id=on_tgt(z + i), device_id_type=MESH)
        return carry

    lax.fori_loop(1, NSRC, greet_src, 0)
    lax.fori_loop(1, NTGT, greet_tgt, 0)

    own = [pltpu.make_async_copy(src_ref, sbuf.at[0], in_sem.at[2])]
    for h in range(2):
        own.append(pltpu.make_async_copy(tgt_ref.at[pl.ds(h * 128, 128)], tbuf.at[chip, core, h], in_sem.at[h]))
    for copy in own:
        copy.start()
    for copy in own:
        copy.wait()

    lane = lax.broadcasted_iota(jnp.int32, (128, 128), 1)
    row = lax.broadcasted_iota(jnp.int32, (128, 128), 0)
    eye = lane == row

    def split3(a):
        a1 = a.astype(BF16).astype(F32)
        rest = a - a1
        a2 = rest.astype(BF16).astype(F32)
        return a1, a2, rest - a2

    def prep_src(d):
        s = sbuf[d]
        scaled = s * (2.0 * ALPHA)
        hi = scaled.astype(BF16)
        lo = (scaled - hi.astype(F32)).astype(BF16)
        b1, b2, b3 = split3(-ALPHA * jnp.sum(s * s, axis=1, keepdims=True))
        extra = jnp.where(lane == 0, b1, jnp.where(lane == 1, b2, jnp.where(lane == 2, b3, jnp.where(lane < 6, 1.0, 0.0))))
        rows = pl.ds(pl.multiple_of((z + d) % NTGT * 128, 128), 128)
        lhs[rows, 0:128] = hi
        lhs[rows, 128:256] = hi
        lhs[rows, 256:384] = lo
        lhs[rows, 384:512] = extra.astype(BF16)

    def prep_tgt(u, q, h):
        for c in range(2):
            t = tbuf[q, c, h]
            pot = pot_ref[pl.ds(q * 4 + c * 2 + h, 1), :]
            hi = t.astype(BF16)
            lo = (t - hi.astype(F32)).astype(BF16)
            a1, a2, a3 = split3(ALPHA * jnp.sum(jnp.where(eye, pot, 0.0) - t * t, axis=1, keepdims=True))
            extra = jnp.where(lane < 3, 1.0, jnp.where(lane == 3, a1, jnp.where(lane == 4, a2, jnp.where(lane == 5, a3, 0.0))))
            rows = pl.ds(c * 128, 128)
            cols[u, rows, 0:128] = lo
            cols[u, rows, 128:256] = hi
            cols[u, rows, 256:384] = hi
            cols[u, rows, 384:512] = extra.astype(BF16)

    prep_src(0)
    top[...] = jnp.full((1024, 128), -jnp.inf, F32)
    total[...] = jnp.zeros((1024, 128), F32)
    pl.semaphore_wait(bar, NSRC + NTGT - 2)

    def at(xx, yy):
        return (((yy + SIDE) % SIDE) * SIDE + (xx + SIDE) % SIDE) * 2 + core

    def step_of(i):
        return (1, -1, 2)[i]

    def p1_copy(h, i):
        step = step_of(i)
        dev = on_src(at(x + step * (1 - h), y + step * h))
        piece = tbuf.at[chip, core, h]
        return rcopy(piece, piece, p1_send.at[h * 3 + i], t_recv.at[h * 16 + chip], dev)

    def z_copy(n):
        up = n % 2 == 0
        sign = 1 if up else -1
        second = n // 2 in (2, 4)
        rows = pl.ds(64 if up == second else 0, 64)
        if n < 2:
            d, to, far, rows = 0, (-sign) % NTGT, 1, pl.ds(0, 128)
        elif n < 6:
            d, to, far = 0, (-2 * sign) % NTGT, 2
        elif n < 10:
            d, to, far = (-2 * sign) % NTGT, (-3 * sign) % NTGT, 1
        else:
            d, to, far = (-2 * sign) % NTGT, 4, 2
        return rcopy(sbuf.at[d, rows], sbuf.at[to, rows], z_send.at[n], z_recv.at[n], on_tgt(z + far * sign))

    for i in range(3):
        for h in range(2):
            p1_copy(h, i).start()
    for n in (2, 3, 4, 5, 0, 1):
        z_copy(n).start()

    def z_near(second):
        for i in range(2):
            n = 2 + 2 * second + i
            z_copy(n).wait_recv()
            z_copy(n + 4).start()
            if not second:
                z_copy(n + 8).start()

    def z_late():
        for n in (0, 1):
            z_copy(n).wait_recv()
        for d in (7, 1, 6, 2):
            prep_src(d)
        for n in range(6, 12):
            z_copy(n).wait_recv()
        for d in (5, 3, 4):
            prep_src(d)

    def place_of(m, h):
        g1 = jnp.where(m < 4, m, (m + 8) // 3 - 4)
        g2 = jnp.where(m < 4, 0, (m + 8) % 3 + 1)
        d1, d2 = gray(g1), gray(g2)
        dx = (1 - h) * d1 + h * d2
        dy = (1 - h) * d2 + h * d1
        return ((y + dy) % SIDE) * SIDE + (x + dx) % SIDE

    def slot_of(u):
        q, h = u // 2, u % 2
        dx = (q % SIDE - x + SIDE) % SIDE
        dy = (q // SIDE - y + SIDE) % SIDE
        g1 = gray(jnp.where(h == 0, dx, dy))
        g2 = gray(jnp.where(h == 0, dy, dx))
        return 2 * jnp.where(g2 == 0, g1, 3 + 3 * g1 + g2) + h

    def p2_copy(m, h, q, i):
        step = step_of(i)
        dev = on_src(at(x + step * h, y + step * (1 - h)))
        piece = tbuf.at[q, core, h]
        return rcopy(piece, piece, p2_send.at[m * 6 + h * 3 + i], t_recv.at[h * 16 + q], dev)

    def sib_copy(m, h, q):
        piece = tbuf.at[q, core, h]
        return rcopy(piece, piece, sib_send.at[m * 2 + h], sib_recv.at[h * 16 + q], on_src(sib))

    def gather_step(m):
        for h in range(2):
            q = place_of(m, h)
            piece = tbuf.at[q, core, h]

            @pl.when(m > 0)
            def _():
                rcopy(piece, piece, sib_send.at[0], t_recv.at[h * 16 + q], on_src(sib)).wait_recv()

            @pl.when(m < 4)
            def _():
                for i in range(3):
                    p2_copy(m, h, q, i).start()

            sib_copy(m, h, q).start()

    def score_rows(us, r0, n):
        for j, u in enumerate(us):
            scores[u, pl.ds(r0, n), :] = lax.dot_general(
                lhs[pl.ds(r0, n), :], cols[u], (((1,), (1,)), ((), ())), preferred_element_type=F32
            )
            if j % 2 == 0:
                continue
            for r in range(r0, r0 + n, 64):
                rows = pl.ds(r, 64)
                parts = [scores[v, rows, pl.ds(k * 128, 128)] for v in (us[j - 1], u) for k in range(2)]
                old = top[rows, :]
                new = old
                for p in parts:
                    new = jnp.maximum(new, p)
                sums = total[rows, :] * jnp.exp2(old - new)
                for p in parts:
                    sums = sums + jnp.exp2(p - new)
                total[rows, :] = sums
                top[rows, :] = new

    def lead(m, carry):
        gather_step(m)

        for n in (1, 2):

            @pl.when(m == n)
            def _():
                z_near(n - 1)

        return carry

    lax.fori_loop(0, 4, lead, 0)
    z_late()

    def first_pass(i, carry):
        for m in (i * 2 + 2, i * 2 + 3):

            @pl.when(jnp.logical_and(m >= 4, m < 16))
            def _():
                gather_step(m)

        for p in (i * 2, i * 2 + 1):
            for h in range(2):
                q = place_of(p, h)
                piece = tbuf.at[q, 1 - core, h]
                rcopy(piece, piece, sib_send.at[0], sib_recv.at[h * 16 + q], on_src(sib)).wait_recv()
        for p in (i * 2, i * 2 + 1):
            for h in range(2):
                prep_tgt(p * 2 + h, place_of(p, h), h)
        score_rows([i * 4 + j for j in range(4)], 0, EARLY * 128)
        return carry

    lax.fori_loop(0, 8, first_pass, 0)

    def r_copy(part, i):
        slot = rslot.at[part, z]
        return rcopy(slot, slot, r_send.at[part * NTGT + i], r_recv.at[part * NTGT + z], on_tgt(z + i))

    def row_sums(part, blocks):
        rslot[part, z] = jnp.zeros((8, 128), F32)
        for c in blocks:
            rows = pl.ds(c * 128, 128)
            m = top[rows, :]
            high = jnp.max(m, axis=1, keepdims=True)
            s = jnp.sum(total[rows, :] * jnp.exp2(m - high), axis=1, keepdims=True)
            r = high + jnp.log2(s)
            rslot[part, z, c : c + 1, :] = jnp.sum(jnp.where(eye, r, 0.0), axis=0, keepdims=True)
        for i in range(1, NTGT):
            r_copy(part, i).start()

    def row_totals(part, blocks):
        for i in range(1, NTGT):
            other = (z + i) % NTGT
            slot = rslot.at[part, other]
            rcopy(slot, slot, r_send.at[0], r_recv.at[part * NTGT + other], on_tgt(z + i)).wait_recv()
        slots = [rslot[part, i] for i in range(NTGT)]
        high = slots[0]
        for s in slots[1:]:
            high = jnp.maximum(high, s)
        sums = jnp.exp2(slots[0] - high)
        for s in slots[1:]:
            sums = sums + jnp.exp2(s - high)
        r_all = high + jnp.log2(sums)
        for c in blocks:
            one = r_all[c : c + 1, :]
            sp_ref[c : c + 1, :] = -epsilon * math.log(NSRC * 1024) - (epsilon * LN2) * one
            rcol[pl.ds(c * 128, 128), :] = jnp.transpose(jnp.broadcast_to(one, (128, 128)))

    early, late = range(EARLY), range(EARLY, 8)
    row_sums(0, early)

    def late_rows(i, carry):
        score_rows([i * 8 + j for j in range(8)], EARLY * 128, 1024 - EARLY * 128)
        return carry

    lax.fori_loop(0, 4, late_rows, 0)
    row_sums(1, late)

    row_totals(0, early)

    def l_copy(u):
        return rcopy(lsend.at[u], lrecv.at[me], l_send.at[u], l_recv.at[me], on_src(u))

    def c_copy(i):
        return rcopy(call.at[me], call.at[me], c_send.at[i], c_recv.at[me], on_src((me + i) % NSRC))

    def column_blocks(slot, blocks):
        b0, n = blocks[0], len(blocks)
        for k in range(2):
            lanes = pl.ds(k * 128, 128)
            tops, sums = [], []
            for b in blocks:
                rows = pl.ds(b * 128, 128)
                v = scores[slot, rows, lanes] - rcol[rows, :]
                q = jnp.max(v, axis=0, keepdims=True)
                e = jnp.exp2(v - q)
                scores[slot, rows, lanes] = e
                tops.append(q)
                sums.append(jnp.sum(e, axis=0, keepdims=True))
            colmax[slot, pl.ds(b0, n), lanes] = jnp.concatenate(tops, axis=0)
            colsum[slot, pl.ds(b0, n), lanes] = jnp.concatenate(sums, axis=0)

    def early_blocks(i, carry):
        for j in range(4):
            column_blocks(i * 4 + j, early)
        return carry

    def late_blocks(i, carry):
        us = (2 * i, 2 * i + 1)
        slots = [slot_of(u) for u in us]
        for slot in slots:
            column_blocks(slot, late)
        for u, slot in zip(us, slots):
            tops = colmax[slot]
            high = jnp.max(tops, axis=0, keepdims=True)
            lsend[u] = high + jnp.log2(jnp.sum(colsum[slot] * jnp.exp2(tops - high), axis=0, keepdims=True))
        for u in us:

            @pl.when(u != me)
            def _():
                l_copy(u).start()

            @pl.when(u == me)
            def _():
                lrecv[me] = lsend[u]

        return carry

    def column_total():
        def arrived(i, carry):
            other = (me + i) % NSRC
            slot = lrecv.at[other]
            rcopy(slot, slot, l_send.at[0], l_recv.at[other], on_src(other)).wait_recv()
            return carry

        lax.fori_loop(1, NSRC, arrived, 0)
        parts = lrecv[...]
        high = jnp.max(parts, axis=0)
        call[me] = high + jnp.log2(jnp.sum(jnp.exp2(parts - high[None]), axis=0))

        def tell(i, carry):
            c_copy(i).start()
            return carry

        lax.fori_loop(1, NSRC, tell, 0)

    lax.fori_loop(0, NSRC // 4, early_blocks, 0)
    row_totals(1, late)
    lax.fori_loop(0, NSRC // 2, late_blocks, 0)

    for h in range(2):
        for i in range(3):
            p1_copy(h, i).wait_send()
    for n in range(12):
        z_copy(n).wait_send()

    def gather_sent(m, carry):
        for h in range(2):
            q = place_of(m, h)

            @pl.when(m < 4)
            def _():
                for i in range(3):
                    p2_copy(m, h, q, i).wait_send()

            sib_copy(m, h, q).wait_send()
        return carry

    lax.fori_loop(0, 16, gather_sent, 0)
    column_total()

    acc[...] = jnp.zeros((1024, 256), F32)
    den[...] = jnp.zeros((1024, 128), F32)

    def map_units(i, dists, wait):
        if wait:
            for j in range(WIDE):
                u = i * WIDE + j

                @pl.when(u != me)
                def _():
                    slot = call.at[u]
                    rcopy(slot, slot, c_send.at[0], c_recv.at[u], on_src(u)).wait_recv()

        high, low, t, sums = [], [], [], None
        for j in range(WIDE):
            u = i * WIDE + j
            slot = slot_of(u)
            ws = []
            for d in dists:
                c = (z + d) % NTGT
                f = jnp.exp2(colmax[slot, pl.ds(c, 1), :] - call[u])
                ws.append(scores[slot, pl.ds(pl.multiple_of(c * 128, 128), 128), :] * f)
            w = jnp.concatenate(ws, axis=0)
            half = w[:, :128] + w[:, 128:]
            sums = half if sums is None else sums + half
            hi = w.astype(BF16)
            high.append(hi)
            low.append((w - hi.astype(F32)).astype(BF16))
            t.append(cols[slot, :, 0:256])
        rows = pl.ds(ORDER.index(dists[0]) * 128, len(dists) * 128)
        den[rows, :] += sums
        acc[rows, :] += jnp.dot(
            jnp.concatenate(high + low, axis=1), jnp.concatenate(t + t, axis=0), preferred_element_type=F32
        )

    def map_rows(dists, wait):
        def body(i, carry):
            map_units(i, dists, wait)
            return carry

        lax.fori_loop(0, NSRC // WIDE, body, 0)

    def block(place):
        rows = pl.ds(place * 128, 128)
        d = jnp.sum(den[rows, :], axis=1, keepdims=True)
        return acc[rows, 0:128] + acc[rows, 128:256], jnp.sum(jnp.where(eye, d, 0.0), axis=0, keepdims=True)

    def z_sum(n):
        sign = 1 if n % 2 == 0 else -1
        rows = pl.ds(0, 136) if n >= 2 else (pl.ds(0, 64) if n == 0 else pl.ds(64, 72))
        far = (2, 1, 2, 1)[n // 2]
        return rcopy(zsend.at[n, rows], zland.at[n, rows], m_send.at[n], m_recv.at[n], on_tgt(z + far * sign))

    def put(n, place):
        num, d = block(place)
        zsend[n, 0:128, :] = num
        zsend[n, 128:136, :] = jnp.broadcast_to(d, (8, 128))

    map_rows(ORDER[0:3], True)
    for n, d in ((0, 4), (1, 4), (2, 3), (3, 5)):
        put(n, ORDER.index(d))
        z_sum(n).start()
    map_rows(ORDER[3:6], False)
    for n, d in ((6, 1), (7, 7)):
        put(n, ORDER.index(d))
        z_sum(n).start()
    map_rows(ORDER[6:8], False)
    for n, d in ((4, 2), (5, 6)):
        put(n, ORDER.index(d))
        for k in (n - 4, n - 2):
            z_sum(k).wait_recv()
        zsend[n] += zland[n - 2]
        part = pl.ds(0, 64) if n == 4 else pl.ds(64, 72)
        zsend[n, part, :] += zland[n - 4, part, :]
        z_sum(n).start()
    own_num, own_den = block(ORDER.index(0))

    for u in range(NSRC):
        for c in range(2):
            r = (u // 2) * 4 + c * 2 + u % 2
            tp_ref[r : r + 1, :] = (
                pot_ref[r : r + 1, :] - (epsilon * LN2) * call[u, :, c * 128 : (c + 1) * 128]
                - epsilon * math.log(NTGT * 8192 / (NSRC * 1024))
            )
    for i in range(1, NTGT):
        for part in range(2):
            r_copy(part, i).wait_send()

    def small_sent(i, carry):
        c_copy(i).wait_send()
        l_copy((me + i) % NSRC).wait_send()
        return carry

    lax.fori_loop(1, NSRC, small_sent, 0)
    for n in range(8):
        z_sum(n).wait_send()
    for n in range(4, 8):
        z_sum(n).wait_recv()
    num = (own_num + (zland[6, 0:128, :] + zland[7, 0:128, :])) + (zland[4, 0:128, :] + zland[5, 0:128, :])
    d = (own_den + (zland[6, 128:129, :] + zland[7, 128:129, :])) + (zland[4, 128:129, :] + zland[5, 128:129, :])
    d = jnp.sum(jnp.where(eye, d, 0.0), axis=1, keepdims=True)
    map_ref[...] = num / d


def finish(sp, tp, mapped, sp_ref, tp_ref, map_ref):
    sp_ref[...] = sp[...]
    tp_ref[...] = tp[...]
    map_ref[...] = mapped[...]


def per_device(sources, targets, potential_in):
    vmem = pl.BlockSpec(memory_space=pltpu.VMEM)
    dma = pltpu.SemaphoreType.DMA
    shapes = (
        jax.ShapeDtypeStruct((8, 128), F32),
        jax.ShapeDtypeStruct((64, 128), F32),
        jax.ShapeDtypeStruct((128, 128), F32),
    )
    results = pl.pallas_call(
        kernel,
        out_shape=shapes,
        in_specs=[pl.BlockSpec(memory_space=pl.ANY)] * 2 + [vmem],
        out_specs=(vmem,) * 3,
        scratch_shapes=[
            pltpu.VMEM((8, 128, 128), F32),
            pltpu.VMEM((16, 2, 2, 128, 128), F32),
            pltpu.VMEM((1024, 512), BF16),
            pltpu.VMEM((32, 256, 512), BF16),
            pltpu.VMEM((32, 1024, 256), F32),
            pltpu.VMEM((1024, 128), F32),
            pltpu.VMEM((1024, 128), F32),
            pltpu.VMEM((2, 8, 8, 128), F32),
            pltpu.VMEM((1024, 128), F32),
            pltpu.VMEM((32, 1, 256), F32),
            pltpu.VMEM((32, 1, 256), F32),
            pltpu.VMEM((32, 1, 256), F32),
            pltpu.VMEM((32, 8, 256), F32),
            pltpu.VMEM((1024, 256), F32),
            pltpu.VMEM((1024, 128), F32),
            pltpu.VMEM((8, 136, 128), F32),
            pltpu.VMEM((8, 136, 128), F32),
            pltpu.VMEM((32, 8, 256), F32),
            dma((3,)),
            dma((12,)),
            dma((16,)),
            dma((6,)),
            dma((24,)),
            dma((32,)),
            dma((32,)),
            dma((32,)),
            dma((16,)),
            dma((16,)),
            dma((32,)),
            dma((32,)),
            dma((32,)),
            dma((32,)),
            dma((8,)),
            dma((8,)),
        ],
        compiler_params=pltpu.CompilerParams(
            collective_id=0, has_side_effects=True, vmem_limit_bytes=62 * 1024 * 1024
        ),
        cost_estimate=pl.CostEstimate(
            flops=2 * 1024 * 8192 * 1024, bytes_accessed=1 << 20, transcendentals=2 * 1024 * 8192
        ),
    )(sources, targets, potential_in.reshape(64, 128))
    sp, tp, mapped = pl.pallas_call(
        finish, out_shape=shapes, in_specs=[vmem] * 3, out_specs=(vmem,) * 3
    )(*results)
    return sp.reshape(1024), tp.reshape(8192), mapped


def solution(mesh):
    return jax.shard_map(
        per_device,
        mesh=mesh,
        in_specs=(P(("src", "tgt"), None), P(("tgt", "src"), None), P("tgt")),
        out_specs=(P("src"), P("tgt"), P(("src", "tgt"), None)),
        check_vma=False,
    )
```

```python
import math

import jax
import jax.numpy as jnp
from jax import lax
from jax.experimental import pallas as pl
from jax.experimental.pallas import tpu as pltpu
from jax.sharding import PartitionSpec as P

epsilon = 0.05
LN2 = math.log(2.0)
ALPHA = 1.0 / (epsilon * LN2)
MESH = pl.DeviceIdType.MESH
F32 = jnp.float32
BF16 = jnp.bfloat16
NSRC = 32
NTGT = 8
ORDER = (4, 3, 5, 1, 7, 2, 6, 0)
SIDE = 4
WIDE = 8
EARLY = 5


def gray(i):
    return i + i // 2 - 2 * (i // 3)


def kernel(
    src_ref, tgt_ref, pot_ref, sp_ref, tp_ref, map_ref,
    sbuf, tbuf, lhs, cols, scores, top, total, rslot, rcol,
    lsend, lrecv, call, colmax, acc, den, zsend, zland, colsum,
    in_sem, z_send, z_recv, p1_send, p2_send, sib_send, t_recv, sib_recv,
    r_send, r_recv, l_send, l_recv, c_send, c_recv, m_send, m_recv,
):
    me = lax.axis_index("src")
    z = lax.axis_index("tgt")
    core = me % 2
    chip = me // 2
    x = chip % SIDE
    y = chip // SIDE
    sib = me + 1 - 2 * core

    def on_src(i):
        return {"src": i}

    def on_tgt(i):
        return {"tgt": (i + NTGT) % NTGT}

    def rcopy(src, dst, send, recv, dev):
        return pltpu.make_async_remote_copy(
            src_ref=src, dst_ref=dst, send_sem=send, recv_sem=recv, device_id=dev, device_id_type=MESH
        )

    bar = pltpu.get_barrier_semaphore()

    def greet_src(i, carry):
        pl.semaphore_signal(bar, inc=1, device_id=on_src((me + i) % NSRC), device_id_type=MESH)
        return carry

    def greet_tgt(i, carry):
        pl.semaphore_signal(bar, inc=1, device_id=on_tgt(z + i), device_id_type=MESH)
        return carry

    lax.fori_loop(1, NSRC, greet_src, 0)
    lax.fori_loop(1, NTGT, greet_tgt, 0)

    own = [pltpu.make_async_copy(src_ref, sbuf.at[0], in_sem.at[2])]
    for h in range(2):
        own.append(pltpu.make_async_copy(tgt_ref.at[pl.ds(h * 128, 128)], tbuf.at[chip, core, h], in_sem.at[h]))
    for copy in own:
        copy.start()
    for copy in own:
        copy.wait()

    lane = lax.broadcasted_iota(jnp.int32, (128, 128), 1)
    row = lax.broadcasted_iota(jnp.int32, (128, 128), 0)
    eye = lane == row

    def split3(a):
        a1 = a.astype(BF16).astype(F32)
        rest = a - a1
        a2 = rest.astype(BF16).astype(F32)
        return a1, a2, rest - a2

    def prep_src(d):
        s = sbuf[d]
        scaled = s * (2.0 * ALPHA)
        hi = scaled.astype(BF16)
        lo = (scaled - hi.astype(F32)).astype(BF16)
        b1, b2, b3 = split3(-ALPHA * jnp.sum(s * s, axis=1, keepdims=True))
        extra = jnp.where(lane == 0, b1, jnp.where(lane == 1, b2, jnp.where(lane == 2, b3, jnp.where(lane < 6, 1.0, 0.0))))
        rows = pl.ds(pl.multiple_of((z + d) % NTGT * 128, 128), 128)
        lhs[rows, 0:128] = hi
        lhs[rows, 128:256] = hi
        lhs[rows, 256:384] = lo
        lhs[rows, 384:512] = extra.astype(BF16)

    def prep_tgt(u, q, h):
        for c in range(2):
            t = tbuf[q, c, h]
            pot = pot_ref[pl.ds(q * 4 + c * 2 + h, 1), :]
            hi = t.astype(BF16)
            lo = (t - hi.astype(F32)).astype(BF16)
            a1, a2, a3 = split3(ALPHA * jnp.sum(jnp.where(eye, pot, 0.0) - t * t, axis=1, keepdims=True))
            extra = jnp.where(lane < 3, 1.0, jnp.where(lane == 3, a1, jnp.where(lane == 4, a2, jnp.where(lane == 5, a3, 0.0))))
            rows = pl.ds(c * 128, 128)
            cols[u, rows, 0:128] = lo
            cols[u, rows, 128:256] = hi
            cols[u, rows, 256:384] = hi
            cols[u, rows, 384:512] = extra.astype(BF16)

    prep_src(0)
    top[...] = jnp.full((1024, 128), -jnp.inf, F32)
    total[...] = jnp.zeros((1024, 128), F32)
    pl.semaphore_wait(bar, NSRC + NTGT - 2)

    def at(xx, yy):
        return (((yy + SIDE) % SIDE) * SIDE + (xx + SIDE) % SIDE) * 2 + core

    def step_of(i):
        return (1, -1, 2)[i]

    def p1_copy(h, i):
        step = step_of(i)
        dev = on_src(at(x + step * (1 - h), y + step * h))
        piece = tbuf.at[chip, core, h]
        return rcopy(piece, piece, p1_send.at[h * 3 + i], t_recv.at[h * 16 + chip], dev)

    def z_copy(n):
        up = n % 2 == 0
        sign = 1 if up else -1
        second = n // 2 in (2, 4)
        rows = pl.ds(64 if up == second else 0, 64)
        if n < 2:
            d, to, far, rows = 0, (-sign) % NTGT, 1, pl.ds(0, 128)
        elif n < 6:
            d, to, far = 0, (-2 * sign) % NTGT, 2
        elif n < 10:
            d, to, far = (-2 * sign) % NTGT, (-3 * sign) % NTGT, 1
        else:
            d, to, far = (-2 * sign) % NTGT, 4, 2
        return rcopy(sbuf.at[d, rows], sbuf.at[to, rows], z_send.at[n], z_recv.at[n], on_tgt(z + far * sign))

    for i in range(3):
        for h in range(2):
            p1_copy(h, i).start()
    for n in (2, 3, 4, 5, 0, 1):
        z_copy(n).start()

    def z_near(second):
        for i in range(2):
            n = 2 + 2 * second + i
            z_copy(n).wait_recv()
            z_copy(n + 4).start()
            if not second:
                z_copy(n + 8).start()

    def z_late():
        for n in (0, 1):
            z_copy(n).wait_recv()
        for d in (7, 1, 6, 2):
            prep_src(d)
        for n in range(6, 12):
            z_copy(n).wait_recv()
        for d in (5, 3, 4):
            prep_src(d)

    def place_of(m, h):
        g1 = jnp.where(m < 4, m, (m + 8) // 3 - 4)
        g2 = jnp.where(m < 4, 0, (m + 8) % 3 + 1)
        d1, d2 = gray(g1), gray(g2)
        dx = (1 - h) * d1 + h * d2
        dy = (1 - h) * d2 + h * d1
        return ((y + dy) % SIDE) * SIDE + (x + dx) % SIDE

    def slot_of(u):
        q, h = u // 2, u % 2
        dx = (q % SIDE - x + SIDE) % SIDE
        dy = (q // SIDE - y + SIDE) % SIDE
        g1 = gray(jnp.where(h == 0, dx, dy))
        g2 = gray(jnp.where(h == 0, dy, dx))
        return 2 * jnp.where(g2 == 0, g1, 3 + 3 * g1 + g2) + h

    def p2_copy(m, h, q, i):
        step = step_of(i)
        dev = on_src(at(x + step * h, y + step * (1 - h)))
        piece = tbuf.at[q, core, h]
        return rcopy(piece, piece, p2_send.at[m * 6 + h * 3 + i], t_recv.at[h * 16 + q], dev)

    def sib_copy(m, h, q):
        piece = tbuf.at[q, core, h]
        return rcopy(piece, piece, sib_send.at[m * 2 + h], sib_recv.at[h * 16 + q], on_src(sib))

    def gather_step(m):
        for h in range(2):
            q = place_of(m, h)
            piece = tbuf.at[q, core, h]

            @pl.when(m > 0)
            def _():
                rcopy(piece, piece, sib_send.at[0], t_recv.at[h * 16 + q], on_src(sib)).wait_recv()

            @pl.when(m < 4)
            def _():
                for i in range(3):
                    p2_copy(m, h, q, i).start()

            sib_copy(m, h, q).start()

    def score_rows(us, r0, n):
        for j, u in enumerate(us):
            scores[u, pl.ds(r0, n), :] = lax.dot_general(
                lhs[pl.ds(r0, n), :], cols[u], (((1,), (1,)), ((), ())), preferred_element_type=F32
            )
            if j % 2 == 0:
                continue
            for r in range(r0, r0 + n, 64):
                rows = pl.ds(r, 64)
                parts = [scores[v, rows, pl.ds(k * 128, 128)] for v in (us[j - 1], u) for k in range(2)]
                old = top[rows, :]
                new = old
                for p in parts:
                    new = jnp.maximum(new, p)
                sums = total[rows, :] * jnp.exp2(old - new)
                for p in parts:
                    sums = sums + jnp.exp2(p - new)
                total[rows, :] = sums
                top[rows, :] = new

    def lead(m, carry):
        gather_step(m)

        for n in (1, 2):

            @pl.when(m == n)
            def _():
                z_near(n - 1)

        return carry

    lax.fori_loop(0, 4, lead, 0)
    z_late()

    def first_pass(i, carry):
        for m in (i * 2 + 2, i * 2 + 3):

            @pl.when(jnp.logical_and(m >= 4, m < 16))
            def _():
                gather_step(m)

        for p in (i * 2, i * 2 + 1):
            for h in range(2):
                q = place_of(p, h)
                piece = tbuf.at[q, 1 - core, h]
                rcopy(piece, piece, sib_send.at[0], sib_recv.at[h * 16 + q], on_src(sib)).wait_recv()
        for p in (i * 2, i * 2 + 1):
            for h in range(2):
                prep_tgt(p * 2 + h, place_of(p, h), h)
        score_rows([i * 4 + j for j in range(4)], 0, EARLY * 128)
        return carry

    lax.fori_loop(0, 8, first_pass, 0)

    def r_copy(part, i):
        slot = rslot.at[part, z]
        return rcopy(slot, slot, r_send.at[part * NTGT + i], r_recv.at[part * NTGT + z], on_tgt(z + i))

    def row_sums(part, blocks):
        rslot[part, z] = jnp.zeros((8, 128), F32)
        for c in blocks:
            rows = pl.ds(c * 128, 128)
            m = top[rows, :]
            high = jnp.max(m, axis=1, keepdims=True)
            s = jnp.sum(total[rows, :] * jnp.exp2(m - high), axis=1, keepdims=True)
            r = high + jnp.log2(s)
            rslot[part, z, c : c + 1, :] = jnp.sum(jnp.where(eye, r, 0.0), axis=0, keepdims=True)
        for i in range(1, NTGT):
            r_copy(part, i).start()

    def row_totals(part, blocks):
        for i in range(1, NTGT):
            other = (z + i) % NTGT
            slot = rslot.at[part, other]
            rcopy(slot, slot, r_send.at[0], r_recv.at[part * NTGT + other], on_tgt(z + i)).wait_recv()
        slots = [rslot[part, i] for i in range(NTGT)]
        high = slots[0]
        for s in slots[1:]:
            high = jnp.maximum(high, s)
        sums = jnp.exp2(slots[0] - high)
        for s in slots[1:]:
            sums = sums + jnp.exp2(s - high)
        r_all = high + jnp.log2(sums)
        for c in blocks:
            one = r_all[c : c + 1, :]
            sp_ref[c : c + 1, :] = -epsilon * math.log(NSRC * 1024) - (epsilon * LN2) * one
            rcol[pl.ds(c * 128, 128), :] = jnp.transpose(jnp.broadcast_to(one, (128, 128)))

    early, late = range(EARLY), range(EARLY, 8)
    row_sums(0, early)

    def late_rows(i, carry):
        score_rows([i * 8 + j for j in range(8)], EARLY * 128, 1024 - EARLY * 128)
        return carry

    lax.fori_loop(0, 4, late_rows, 0)
    row_sums(1, late)

    row_totals(0, early)

    def l_copy(u):
        return rcopy(lsend.at[u], lrecv.at[me], l_send.at[u], l_recv.at[me], on_src(u))

    def c_copy(i):
        return rcopy(call.at[me], call.at[me], c_send.at[i], c_recv.at[me], on_src((me + i) % NSRC))

    def column_blocks(slot, blocks):
        b0, n = blocks[0], len(blocks)
        for k in range(2):
            lanes = pl.ds(k * 128, 128)
            tops, sums = [], []
            for b in blocks:
                rows = pl.ds(b * 128, 128)
                v = scores[slot, rows, lanes] - rcol[rows, :]
                q = jnp.max(v, axis=0, keepdims=True)
                e = jnp.exp2(v - q)
                scores[slot, rows, lanes] = e
                tops.append(q)
                sums.append(jnp.sum(e, axis=0, keepdims=True))
            colmax[slot, pl.ds(b0, n), lanes] = jnp.concatenate(tops, axis=0)
            colsum[slot, pl.ds(b0, n), lanes] = jnp.concatenate(sums, axis=0)

    def early_blocks(i, carry):
        for j in range(4):
            column_blocks(i * 4 + j, early)
        return carry

    def late_blocks(i, carry):
        us = (2 * i, 2 * i + 1)
        slots = [slot_of(u) for u in us]
        for slot in slots:
            column_blocks(slot, late)
        for u, slot in zip(us, slots):
            tops = colmax[slot]
            high = jnp.max(tops, axis=0, keepdims=True)
            lsend[u] = high + jnp.log2(jnp.sum(colsum[slot] * jnp.exp2(tops - high), axis=0, keepdims=True))
        for u in us:

            @pl.when(u != me)
            def _():
                l_copy(u).start()

            @pl.when(u == me)
            def _():
                lrecv[me] = lsend[u]

        return carry

    def column_total():
        def arrived(i, carry):
            other = (me + i) % NSRC
            slot = lrecv.at[other]
            rcopy(slot, slot, l_send.at[0], l_recv.at[other], on_src(other)).wait_recv()
            return carry

        lax.fori_loop(1, NSRC, arrived, 0)
        parts = lrecv[...]
        high = jnp.max(parts, axis=0)
        call[me] = high + jnp.log2(jnp.sum(jnp.exp2(parts - high[None]), axis=0))

        def tell(i, carry):
            c_copy(i).start()
            return carry

        lax.fori_loop(1, NSRC, tell, 0)

    lax.fori_loop(0, NSRC // 4, early_blocks, 0)
    row_totals(1, late)
    lax.fori_loop(0, NSRC // 2, late_blocks, 0)

    for h in range(2):
        for i in range(3):
            p1_copy(h, i).wait_send()
    for n in range(12):
        z_copy(n).wait_send()

    def gather_sent(m, carry):
        for h in range(2):
            q = place_of(m, h)

            @pl.when(m < 4)
            def _():
                for i in range(3):
                    p2_copy(m, h, q, i).wait_send()

            sib_copy(m, h, q).wait_send()
        return carry

    lax.fori_loop(0, 16, gather_sent, 0)
    column_total()

    acc[...] = jnp.zeros((1024, 256), F32)
    den[...] = jnp.zeros((1024, 128), F32)

    def map_units(i, dists, wait):
        if wait:
            for j in range(WIDE):
                u = i * WIDE + j

                @pl.when(u != me)
                def _():
                    slot = call.at[u]
                    rcopy(slot, slot, c_send.at[0], c_recv.at[u], on_src(u)).wait_recv()

        high, low, t, sums = [], [], [], None
        for j in range(WIDE):
            u = i * WIDE + j
            slot = slot_of(u)
            ws = []
            for d in dists:
                c = (z + d) % NTGT
                f = jnp.exp2(colmax[slot, pl.ds(c, 1), :] - call[u])
                ws.append(scores[slot, pl.ds(pl.multiple_of(c * 128, 128), 128), :] * f)
            w = jnp.concatenate(ws, axis=0)
            half = w[:, :128] + w[:, 128:]
            sums = half if sums is None else sums + half
            hi = w.astype(BF16)
            high.append(hi)
            low.append((w - hi.astype(F32)).astype(BF16))
            t.append(cols[slot, :, 0:256])
        rows = pl.ds(ORDER.index(dists[0]) * 128, len(dists) * 128)
        den[rows, :] += sums
        acc[rows, :] += jnp.dot(
            jnp.concatenate(high + low, axis=1), jnp.concatenate(t + t, axis=0), preferred_element_type=F32
        )

    def map_rows(dists, wait):
        def body(i, carry):
            map_units(i, dists, wait)
            return carry

        lax.fori_loop(0, NSRC // WIDE, body, 0)

    def block(place):
        rows = pl.ds(place * 128, 128)
        d = jnp.sum(den[rows, :], axis=1, keepdims=True)
        return acc[rows, 0:128] + acc[rows, 128:256], jnp.sum(jnp.where(eye, d, 0.0), axis=0, keepdims=True)

    def z_sum(n):
        sign = 1 if n % 2 == 0 else -1
        rows = pl.ds(0, 136) if n >= 2 else (pl.ds(0, 64) if n == 0 else pl.ds(64, 72))
        far = (2, 1, 2, 1)[n // 2]
        return rcopy(zsend.at[n, rows], zland.at[n, rows], m_send.at[n], m_recv.at[n], on_tgt(z + far * sign))

    def put(n, place):
        num, d = block(place)
        zsend[n, 0:128, :] = num
        zsend[n, 128:136, :] = jnp.broadcast_to(d, (8, 128))

    map_rows(ORDER[0:3], True)
    for n, d in ((0, 4), (1, 4), (2, 3), (3, 5)):
        put(n, ORDER.index(d))
        z_sum(n).start()
    map_rows(ORDER[3:5], False)
    for n, d in ((6, 1), (7, 7)):
        put(n, ORDER.index(d))
        z_sum(n).start()
    map_rows(ORDER[5:7], False)
    for n, d in ((4, 2), (5, 6)):
        put(n, ORDER.index(d))
        for k in (n - 4, n - 2):
            z_sum(k).wait_recv()
        zsend[n] += zland[n - 2]
        part = pl.ds(0, 64) if n == 4 else pl.ds(64, 72)
        zsend[n, part, :] += zland[n - 4, part, :]
        z_sum(n).start()
    map_rows(ORDER[7:8], False)
    own_num, own_den = block(ORDER.index(0))

    for u in range(NSRC):
        for c in range(2):
            r = (u // 2) * 4 + c * 2 + u % 2
            tp_ref[r : r + 1, :] = (
                pot_ref[r : r + 1, :] - (epsilon * LN2) * call[u, :, c * 128 : (c + 1) * 128]
                - epsilon * math.log(NTGT * 8192 / (NSRC * 1024))
            )
    for i in range(1, NTGT):
        for part in range(2):
            r_copy(part, i).wait_send()

    def small_sent(i, carry):
        c_copy(i).wait_send()
        l_copy((me + i) % NSRC).wait_send()
        return carry

    lax.fori_loop(1, NSRC, small_sent, 0)
    for n in range(8):
        z_sum(n).wait_send()
    for n in range(4, 8):
        z_sum(n).wait_recv()
    num = (own_num + (zland[6, 0:128, :] + zland[7, 0:128, :])) + (zland[4, 0:128, :] + zland[5, 0:128, :])
    d = (own_den + (zland[6, 128:129, :] + zland[7, 128:129, :])) + (zland[4, 128:129, :] + zland[5, 128:129, :])
    d = jnp.sum(jnp.where(eye, d, 0.0), axis=1, keepdims=True)
    map_ref[...] = num / d


def finish(sp, tp, mapped, sp_ref, tp_ref, map_ref):
    sp_ref[...] = sp[...]
    tp_ref[...] = tp[...]
    map_ref[...] = mapped[...]


def per_device(sources, targets, potential_in):
    vmem = pl.BlockSpec(memory_space=pltpu.VMEM)
    dma = pltpu.SemaphoreType.DMA
    shapes = (
        jax.ShapeDtypeStruct((8, 128), F32),
        jax.ShapeDtypeStruct((64, 128), F32),
        jax.ShapeDtypeStruct((128, 128), F32),
    )
    results = pl.pallas_call(
        kernel,
        out_shape=shapes,
        in_specs=[pl.BlockSpec(memory_space=pl.ANY)] * 2 + [vmem],
        out_specs=(vmem,) * 3,
        scratch_shapes=[
            pltpu.VMEM((8, 128, 128), F32),
            pltpu.VMEM((16, 2, 2, 128, 128), F32),
            pltpu.VMEM((1024, 512), BF16),
            pltpu.VMEM((32, 256, 512), BF16),
            pltpu.VMEM((32, 1024, 256), F32),
            pltpu.VMEM((1024, 128), F32),
            pltpu.VMEM((1024, 128), F32),
            pltpu.VMEM((2, 8, 8, 128), F32),
            pltpu.VMEM((1024, 128), F32),
            pltpu.VMEM((32, 1, 256), F32),
            pltpu.VMEM((32, 1, 256), F32),
            pltpu.VMEM((32, 1, 256), F32),
            pltpu.VMEM((32, 8, 256), F32),
            pltpu.VMEM((1024, 256), F32),
            pltpu.VMEM((1024, 128), F32),
            pltpu.VMEM((8, 136, 128), F32),
            pltpu.VMEM((8, 136, 128), F32),
            pltpu.VMEM((32, 8, 256), F32),
            dma((3,)),
            dma((12,)),
            dma((16,)),
            dma((6,)),
            dma((24,)),
            dma((32,)),
            dma((32,)),
            dma((32,)),
            dma((16,)),
            dma((16,)),
            dma((32,)),
            dma((32,)),
            dma((32,)),
            dma((32,)),
            dma((8,)),
            dma((8,)),
        ],
        compiler_params=pltpu.CompilerParams(
            collective_id=0, has_side_effects=True, vmem_limit_bytes=62 * 1024 * 1024
        ),
        cost_estimate=pl.CostEstimate(
            flops=2 * 1024 * 8192 * 1024, bytes_accessed=1 << 20, transcendentals=2 * 1024 * 8192
        ),
    )(sources, targets, potential_in.reshape(64, 128))
    sp, tp, mapped = pl.pallas_call(
        finish, out_shape=shapes, in_specs=[vmem] * 3, out_specs=(vmem,) * 3
    )(*results)
    return sp.reshape(1024), tp.reshape(8192), mapped


def solution(mesh):
    return jax.shard_map(
        per_device,
        mesh=mesh,
        in_specs=(P(("src", "tgt"), None), P(("tgt", "src"), None), P("tgt")),
        out_specs=(P("src"), P("tgt"), P(("src", "tgt"), None)),
        check_vma=False,
    )
```

```python
import math

import jax
import jax.numpy as jnp
from jax import lax
from jax.experimental import pallas as pl
from jax.experimental.pallas import tpu as pltpu
from jax.sharding import PartitionSpec as P

epsilon = 0.05
LN2 = math.log(2.0)
ALPHA = 1.0 / (epsilon * LN2)
MESH = pl.DeviceIdType.MESH
F32 = jnp.float32
BF16 = jnp.bfloat16
NSRC = 32
NTGT = 8
ORDER = (4, 3, 5, 1, 7, 2, 6, 0)
SIDE = 4
WIDE = 8
EARLY = 5


def gray(i):
    return i + i // 2 - 2 * (i // 3)


def kernel(
    src_ref, tgt_ref, pot_ref, sp_ref, tp_ref, map_ref,
    sbuf, tbuf, lhs, cols, scores, top, total, rslot, rcol,
    lsend, lrecv, call, colmax, acc, den, zsend, zland, colsum,
    in_sem, z_send, z_recv, p1_send, p2_send, sib_send, t_recv, sib_recv,
    r_send, r_recv, l_send, l_recv, c_send, c_recv, m_send, m_recv,
):
    me = lax.axis_index("src")
    z = lax.axis_index("tgt")
    core = me % 2
    chip = me // 2
    x = chip % SIDE
    y = chip // SIDE
    sib = me + 1 - 2 * core

    def on_src(i):
        return {"src": i}

    def on_tgt(i):
        return {"tgt": (i + NTGT) % NTGT}

    def rcopy(src, dst, send, recv, dev):
        return pltpu.make_async_remote_copy(
            src_ref=src, dst_ref=dst, send_sem=send, recv_sem=recv, device_id=dev, device_id_type=MESH
        )

    bar = pltpu.get_barrier_semaphore()

    def greet_src(i, carry):
        pl.semaphore_signal(bar, inc=1, device_id=on_src((me + i) % NSRC), device_id_type=MESH)
        return carry

    def greet_tgt(i, carry):
        pl.semaphore_signal(bar, inc=1, device_id=on_tgt(z + i), device_id_type=MESH)
        return carry

    lax.fori_loop(1, NSRC, greet_src, 0)
    lax.fori_loop(1, NTGT, greet_tgt, 0)

    own = [pltpu.make_async_copy(src_ref, sbuf.at[0], in_sem.at[2])]
    for h in range(2):
        own.append(pltpu.make_async_copy(tgt_ref.at[pl.ds(h * 128, 128)], tbuf.at[chip, core, h], in_sem.at[h]))
    for copy in own:
        copy.start()
    for copy in own:
        copy.wait()

    lane = lax.broadcasted_iota(jnp.int32, (128, 128), 1)
    row = lax.broadcasted_iota(jnp.int32, (128, 128), 0)
    eye = lane == row

    def split3(a):
        a1 = a.astype(BF16).astype(F32)
        rest = a - a1
        a2 = rest.astype(BF16).astype(F32)
        return a1, a2, rest - a2

    def prep_src(d):
        s = sbuf[d]
        scaled = s * (2.0 * ALPHA)
        hi = scaled.astype(BF16)
        lo = (scaled - hi.astype(F32)).astype(BF16)
        b1, b2, b3 = split3(-ALPHA * jnp.sum(s * s, axis=1, keepdims=True))
        extra = jnp.where(lane == 0, b1, jnp.where(lane == 1, b2, jnp.where(lane == 2, b3, jnp.where(lane < 6, 1.0, 0.0))))
        rows = pl.ds(pl.multiple_of((z + d) % NTGT * 128, 128), 128)
        lhs[rows, 0:128] = hi
        lhs[rows, 128:256] = hi
        lhs[rows, 256:384] = lo
        lhs[rows, 384:512] = extra.astype(BF16)

    def prep_tgt(u, q, h):
        for c in range(2):
            t = tbuf[q, c, h]
            pot = pot_ref[pl.ds(q * 4 + c * 2 + h, 1), :]
            hi = t.astype(BF16)
            lo = (t - hi.astype(F32)).astype(BF16)
            a1, a2, a3 = split3(ALPHA * jnp.sum(jnp.where(eye, pot, 0.0) - t * t, axis=1, keepdims=True))
            extra = jnp.where(lane < 3, 1.0, jnp.where(lane == 3, a1, jnp.where(lane == 4, a2, jnp.where(lane == 5, a3, 0.0))))
            rows = pl.ds(c * 128, 128)
            cols[u, rows, 0:128] = lo
            cols[u, rows, 128:256] = hi
            cols[u, rows, 256:384] = hi
            cols[u, rows, 384:512] = extra.astype(BF16)

    prep_src(0)
    top[...] = jnp.full((1024, 128), -jnp.inf, F32)
    total[...] = jnp.zeros((1024, 128), F32)
    pl.semaphore_wait(bar, NSRC + NTGT - 2)

    def at(xx, yy):
        return (((yy + SIDE) % SIDE) * SIDE + (xx + SIDE) % SIDE) * 2 + core

    def step_of(i):
        return (1, -1, 2)[i]

    def p1_copy(h, i):
        step = step_of(i)
        dev = on_src(at(x + step * (1 - h), y + step * h))
        piece = tbuf.at[chip, core, h]
        return rcopy(piece, piece, p1_send.at[h * 3 + i], t_recv.at[h * 16 + chip], dev)

    def z_copy(n):
        up = n % 2 == 0
        sign = 1 if up else -1
        second = n // 2 in (2, 4)
        rows = pl.ds(64 if up == second else 0, 64)
        if n < 2:
            d, to, far, rows = 0, (-sign) % NTGT, 1, pl.ds(0, 128)
        elif n < 6:
            d, to, far = 0, (-2 * sign) % NTGT, 2
        elif n < 10:
            d, to, far = (-2 * sign) % NTGT, (-3 * sign) % NTGT, 1
        else:
            d, to, far = (-2 * sign) % NTGT, 4, 2
        return rcopy(sbuf.at[d, rows], sbuf.at[to, rows], z_send.at[n], z_recv.at[n], on_tgt(z + far * sign))

    for i in range(3):
        for h in range(2):
            p1_copy(h, i).start()
    for n in (2, 3, 4, 5, 0, 1):
        z_copy(n).start()

    def z_near(second):
        for i in range(2):
            n = 2 + 2 * second + i
            z_copy(n).wait_recv()
            z_copy(n + 4).start()
            if not second:
                z_copy(n + 8).start()

    def z_late():
        for n in (0, 1):
            z_copy(n).wait_recv()
        for d in (7, 1, 6, 2):
            prep_src(d)
        for n in range(6, 12):
            z_copy(n).wait_recv()
        for d in (5, 3, 4):
            prep_src(d)

    def place_of(m, h):
        g1 = jnp.where(m < 4, m, (m + 8) // 3 - 4)
        g2 = jnp.where(m < 4, 0, (m + 8) % 3 + 1)
        d1, d2 = gray(g1), gray(g2)
        dx = (1 - h) * d1 + h * d2
        dy = (1 - h) * d2 + h * d1
        return ((y + dy) % SIDE) * SIDE + (x + dx) % SIDE

    def slot_of(u):
        q, h = u // 2, u % 2
        dx = (q % SIDE - x + SIDE) % SIDE
        dy = (q // SIDE - y + SIDE) % SIDE
        g1 = gray(jnp.where(h == 0, dx, dy))
        g2 = gray(jnp.where(h == 0, dy, dx))
        return 2 * jnp.where(g2 == 0, g1, 3 + 3 * g1 + g2) + h

    def p2_copy(m, h, q, i):
        step = step_of(i)
        dev = on_src(at(x + step * h, y + step * (1 - h)))
        piece = tbuf.at[q, core, h]
        return rcopy(piece, piece, p2_send.at[m * 6 + h * 3 + i], t_recv.at[h * 16 + q], dev)

    def sib_copy(m, h, q):
        piece = tbuf.at[q, core, h]
        return rcopy(piece, piece, sib_send.at[m * 2 + h], sib_recv.at[h * 16 + q], on_src(sib))

    def gather_step(m):
        for h in range(2):
            q = place_of(m, h)
            piece = tbuf.at[q, core, h]

            @pl.when(m > 0)
            def _():
                rcopy(piece, piece, sib_send.at[0], t_recv.at[h * 16 + q], on_src(sib)).wait_recv()

            @pl.when(m < 4)
            def _():
                for i in range(3):
                    p2_copy(m, h, q, i).start()

            sib_copy(m, h, q).start()

    def score_rows(us, r0, n):
        for j, u in enumerate(us):
            scores[u, pl.ds(r0, n), :] = lax.dot_general(
                lhs[pl.ds(r0, n), :], cols[u], (((1,), (1,)), ((), ())), preferred_element_type=F32
            )
            if j % 2 == 0:
                continue
            for r in range(r0, r0 + n, 64):
                rows = pl.ds(r, 64)
                parts = [scores[v, rows, pl.ds(k * 128, 128)] for v in (us[j - 1], u) for k in range(2)]
                old = top[rows, :]
                new = old
                for p in parts:
                    new = jnp.maximum(new, p)
                sums = total[rows, :] * jnp.exp2(old - new)
                for p in parts:
                    sums = sums + jnp.exp2(p - new)
                total[rows, :] = sums
                top[rows, :] = new

    def lead(m, carry):
        gather_step(m)

        for n in (1, 2):

            @pl.when(m == n)
            def _():
                z_near(n - 1)

        return carry

    lax.fori_loop(0, 4, lead, 0)
    z_late()

    def first_pass(i, carry):
        for m in (i * 2 + 2, i * 2 + 3):

            @pl.when(jnp.logical_and(m >= 4, m < 16))
            def _():
                gather_step(m)

        for p in (i * 2, i * 2 + 1):
            for h in range(2):
                q = place_of(p, h)
                piece = tbuf.at[q, 1 - core, h]
                rcopy(piece, piece, sib_send.at[0], sib_recv.at[h * 16 + q], on_src(sib)).wait_recv()
        for p in (i * 2, i * 2 + 1):
            for h in range(2):
                prep_tgt(p * 2 + h, place_of(p, h), h)
        score_rows([i * 4 + j for j in range(4)], 0, EARLY * 128)
        return carry

    lax.fori_loop(0, 8, first_pass, 0)

    def r_copy(part, i):
        slot = rslot.at[part, z]
        return rcopy(slot, slot, r_send.at[part * NTGT + i], r_recv.at[part * NTGT + z], on_tgt(z + i))

    def row_sums(part, blocks):
        rslot[part, z] = jnp.zeros((8, 128), F32)
        for c in blocks:
            rows = pl.ds(c * 128, 128)
            m = top[rows, :]
            high = jnp.max(m, axis=1, keepdims=True)
            s = jnp.sum(total[rows, :] * jnp.exp2(m - high), axis=1, keepdims=True)
            r = high + jnp.log2(s)
            rslot[part, z, c : c + 1, :] = jnp.sum(jnp.where(eye, r, 0.0), axis=0, keepdims=True)
        for i in range(1, NTGT):
            r_copy(part, i).start()

    def row_totals(part, blocks):
        for i in range(1, NTGT):
            other = (z + i) % NTGT
            slot = rslot.at[part, other]
            rcopy(slot, slot, r_send.at[0], r_recv.at[part * NTGT + other], on_tgt(z + i)).wait_recv()
        slots = [rslot[part, i] for i in range(NTGT)]
        high = slots[0]
        for s in slots[1:]:
            high = jnp.maximum(high, s)
        sums = jnp.exp2(slots[0] - high)
        for s in slots[1:]:
            sums = sums + jnp.exp2(s - high)
        r_all = high + jnp.log2(sums)
        for c in blocks:
            one = r_all[c : c + 1, :]
            sp_ref[c : c + 1, :] = -epsilon * math.log(NSRC * 1024) - (epsilon * LN2) * one
            rcol[pl.ds(c * 128, 128), :] = jnp.transpose(jnp.broadcast_to(one, (128, 128)))

    early, late = range(EARLY), range(EARLY, 8)
    row_sums(0, early)

    def late_rows(i, carry):
        score_rows([i * 8 + j for j in range(8)], EARLY * 128, 1024 - EARLY * 128)
        return carry

    lax.fori_loop(0, 4, late_rows, 0)
    row_sums(1, late)

    row_totals(0, early)

    def l_copy(u):
        return rcopy(lsend.at[u], lrecv.at[me], l_send.at[u], l_recv.at[0], on_src(u))

    def c_copy(i):
        return rcopy(call.at[me], call.at[me], c_send.at[i], c_recv.at[me], on_src((me + i) % NSRC))

    def column_blocks(slot, blocks):
        b0, n = blocks[0], len(blocks)
        for k in range(2):
            lanes = pl.ds(k * 128, 128)
            tops, sums = [], []
            for b in blocks:
                rows = pl.ds(b * 128, 128)
                v = scores[slot, rows, lanes] - rcol[rows, :]
                q = jnp.max(v, axis=0, keepdims=True)
                e = jnp.exp2(v - q)
                scores[slot, rows, lanes] = e
                tops.append(q)
                sums.append(jnp.sum(e, axis=0, keepdims=True))
            colmax[slot, pl.ds(b0, n), lanes] = jnp.concatenate(tops, axis=0)
            colsum[slot, pl.ds(b0, n), lanes] = jnp.concatenate(sums, axis=0)

    def early_blocks(i, carry):
        for j in range(4):
            column_blocks(i * 4 + j, early)
        return carry

    def late_blocks(i, carry):
        us = (2 * i, 2 * i + 1)
        slots = [slot_of(u) for u in us]
        for slot in slots:
            column_blocks(slot, late)
        for u, slot in zip(us, slots):
            tops = colmax[slot]
            high = jnp.max(tops, axis=0, keepdims=True)
            lsend[u] = high + jnp.log2(jnp.sum(colsum[slot] * jnp.exp2(tops - high), axis=0, keepdims=True))
        for u in us:

            @pl.when(u != me)
            def _():
                l_copy(u).start()

            @pl.when(u == me)
            def _():
                lrecv[me] = lsend[u]

        return carry

    def column_total():
        others = lrecv.at[pl.ds(0, NSRC - 1)]
        rcopy(others, others, l_send.at[0], l_recv.at[0], on_src(sib)).wait_recv()
        parts = lrecv[...]
        high = jnp.max(parts, axis=0)
        call[me] = high + jnp.log2(jnp.sum(jnp.exp2(parts - high[None]), axis=0))

        def tell(i, carry):
            c_copy(i).start()
            return carry

        lax.fori_loop(1, NSRC, tell, 0)

    lax.fori_loop(0, NSRC // 4, early_blocks, 0)
    row_totals(1, late)
    lax.fori_loop(0, NSRC // 2, late_blocks, 0)

    for h in range(2):
        for i in range(3):
            p1_copy(h, i).wait_send()
    for n in range(12):
        z_copy(n).wait_send()

    def gather_sent(m, carry):
        for h in range(2):
            q = place_of(m, h)

            @pl.when(m < 4)
            def _():
                for i in range(3):
                    p2_copy(m, h, q, i).wait_send()

            sib_copy(m, h, q).wait_send()
        return carry

    lax.fori_loop(0, 16, gather_sent, 0)
    column_total()

    acc[...] = jnp.zeros((1024, 256), F32)
    den[...] = jnp.zeros((1024, 128), F32)

    def map_units(i, dists, wait):
        if wait:
            for j in range(WIDE):
                u = i * WIDE + j

                @pl.when(u != me)
                def _():
                    slot = call.at[u]
                    rcopy(slot, slot, c_send.at[0], c_recv.at[u], on_src(u)).wait_recv()

        high, low, t, sums = [], [], [], None
        for j in range(WIDE):
            u = i * WIDE + j
            slot = slot_of(u)
            ws = []
            for d in dists:
                c = (z + d) % NTGT
                f = jnp.exp2(colmax[slot, pl.ds(c, 1), :] - call[u])
                ws.append(scores[slot, pl.ds(pl.multiple_of(c * 128, 128), 128), :] * f)
            w = jnp.concatenate(ws, axis=0)
            half = w[:, :128] + w[:, 128:]
            sums = half if sums is None else sums + half
            hi = w.astype(BF16)
            high.append(hi)
            low.append((w - hi.astype(F32)).astype(BF16))
            t.append(cols[slot, :, 0:256])
        rows = pl.ds(ORDER.index(dists[0]) * 128, len(dists) * 128)
        den[rows, :] += sums
        acc[rows, :] += jnp.dot(
            jnp.concatenate(high + low, axis=1), jnp.concatenate(t + t, axis=0), preferred_element_type=F32
        )

    def map_rows(dists, wait):
        def body(i, carry):
            map_units(i, dists, wait)
            return carry

        lax.fori_loop(0, NSRC // WIDE, body, 0)

    def block(place):
        rows = pl.ds(place * 128, 128)
        d = jnp.sum(den[rows, :], axis=1, keepdims=True)
        return acc[rows, 0:128] + acc[rows, 128:256], jnp.sum(jnp.where(eye, d, 0.0), axis=0, keepdims=True)

    def z_sum(n):
        sign = 1 if n % 2 == 0 else -1
        rows = pl.ds(0, 136) if n >= 2 else (pl.ds(0, 64) if n == 0 else pl.ds(64, 72))
        far = (2, 1, 2, 1)[n // 2]
        return rcopy(zsend.at[n, rows], zland.at[n, rows], m_send.at[n], m_recv.at[n], on_tgt(z + far * sign))

    def put(n, place):
        num, d = block(place)
        zsend[n, 0:128, :] = num
        zsend[n, 128:136, :] = jnp.broadcast_to(d, (8, 128))

    map_rows(ORDER[0:3], True)
    for n, d in ((0, 4), (1, 4), (2, 3), (3, 5)):
        put(n, ORDER.index(d))
        z_sum(n).start()
    map_rows(ORDER[3:5], False)
    for n, d in ((6, 1), (7, 7)):
        put(n, ORDER.index(d))
        z_sum(n).start()
    map_rows(ORDER[5:7], False)
    for n, d in ((4, 2), (5, 6)):
        put(n, ORDER.index(d))
        for k in (n - 4, n - 2):
            z_sum(k).wait_recv()
        zsend[n] += zland[n - 2]
        part = pl.ds(0, 64) if n == 4 else pl.ds(64, 72)
        zsend[n, part, :] += zland[n - 4, part, :]
        z_sum(n).start()
    map_rows(ORDER[7:8], False)
    own_num, own_den = block(ORDER.index(0))

    for u in range(NSRC):
        for c in range(2):
            r = (u // 2) * 4 + c * 2 + u % 2
            tp_ref[r : r + 1, :] = (
                pot_ref[r : r + 1, :] - (epsilon * LN2) * call[u, :, c * 128 : (c + 1) * 128]
                - epsilon * math.log(NTGT * 8192 / (NSRC * 1024))
            )
    for i in range(1, NTGT):
        for part in range(2):
            r_copy(part, i).wait_send()

    def small_sent(i, carry):
        c_copy(i).wait_send()
        l_copy((me + i) % NSRC).wait_send()
        return carry

    lax.fori_loop(1, NSRC, small_sent, 0)
    for n in range(8):
        z_sum(n).wait_send()
    for n in range(4, 8):
        z_sum(n).wait_recv()
    num = (own_num + (zland[6, 0:128, :] + zland[7, 0:128, :])) + (zland[4, 0:128, :] + zland[5, 0:128, :])
    d = (own_den + (zland[6, 128:129, :] + zland[7, 128:129, :])) + (zland[4, 128:129, :] + zland[5, 128:129, :])
    d = jnp.sum(jnp.where(eye, d, 0.0), axis=1, keepdims=True)
    map_ref[...] = num / d


def finish(sp, tp, mapped, sp_ref, tp_ref, map_ref):
    sp_ref[...] = sp[...]
    tp_ref[...] = tp[...]
    map_ref[...] = mapped[...]


def per_device(sources, targets, potential_in):
    vmem = pl.BlockSpec(memory_space=pltpu.VMEM)
    dma = pltpu.SemaphoreType.DMA
    shapes = (
        jax.ShapeDtypeStruct((8, 128), F32),
        jax.ShapeDtypeStruct((64, 128), F32),
        jax.ShapeDtypeStruct((128, 128), F32),
    )
    results = pl.pallas_call(
        kernel,
        out_shape=shapes,
        in_specs=[pl.BlockSpec(memory_space=pl.ANY)] * 2 + [vmem],
        out_specs=(vmem,) * 3,
        scratch_shapes=[
            pltpu.VMEM((8, 128, 128), F32),
            pltpu.VMEM((16, 2, 2, 128, 128), F32),
            pltpu.VMEM((1024, 512), BF16),
            pltpu.VMEM((32, 256, 512), BF16),
            pltpu.VMEM((32, 1024, 256), F32),
            pltpu.VMEM((1024, 128), F32),
            pltpu.VMEM((1024, 128), F32),
            pltpu.VMEM((2, 8, 8, 128), F32),
            pltpu.VMEM((1024, 128), F32),
            pltpu.VMEM((32, 1, 256), F32),
            pltpu.VMEM((32, 1, 256), F32),
            pltpu.VMEM((32, 1, 256), F32),
            pltpu.VMEM((32, 8, 256), F32),
            pltpu.VMEM((1024, 256), F32),
            pltpu.VMEM((1024, 128), F32),
            pltpu.VMEM((8, 136, 128), F32),
            pltpu.VMEM((8, 136, 128), F32),
            pltpu.VMEM((32, 8, 256), F32),
            dma((3,)),
            dma((12,)),
            dma((16,)),
            dma((6,)),
            dma((24,)),
            dma((32,)),
            dma((32,)),
            dma((32,)),
            dma((16,)),
            dma((16,)),
            dma((32,)),
            dma((1,)),
            dma((32,)),
            dma((32,)),
            dma((8,)),
            dma((8,)),
        ],
        compiler_params=pltpu.CompilerParams(
            collective_id=0, has_side_effects=True, vmem_limit_bytes=62 * 1024 * 1024
        ),
        cost_estimate=pl.CostEstimate(
            flops=2 * 1024 * 8192 * 1024, bytes_accessed=1 << 20, transcendentals=2 * 1024 * 8192
        ),
    )(sources, targets, potential_in.reshape(64, 128))
    sp, tp, mapped = pl.pallas_call(
        finish, out_shape=shapes, in_specs=[vmem] * 3, out_specs=(vmem,) * 3
    )(*results)
    return sp.reshape(1024), tp.reshape(8192), mapped


def solution(mesh):
    return jax.shard_map(
        per_device,
        mesh=mesh,
        in_specs=(P(("src", "tgt"), None), P(("tgt", "src"), None), P("tgt")),
        out_specs=(P("src"), P("tgt"), P(("src", "tgt"), None)),
        check_vma=False,
    )
```
